32 devices in a mesh: expert: 8 (over z, core), tensor: 4 (over y, x).
Axes of the slice: x: 2, y: 2, z: 4, core: 2. Of those that a mesh axis runs over, the one named last changes fastest.
Arguments:
- grad_out: bfloat16 [4096, 2560], P(('expert', 'tensor')), may hold values from -6 to 6
- router_score: bfloat16 [4096], P(('expert', 'tensor')), may hold values from 0.19921875 to 1
- routing: int32 [4096, 1], P(('expert', 'tensor')), may hold values from 0 to 7; in each aligned block of 128 rows (0 to 127, 128 to 255, ...) at most 20 rows name the same one
- gate_pre: bfloat16 [8, 640, 4096], P('expert', None, 'tensor'), may hold values from -6 to 6
- up_pre: bfloat16 [8, 640, 4096], P('expert', None, 'tensor'), may hold values from -6 to 6
- gate_weight: bfloat16 [8, 2560, 4096], P('expert', None, 'tensor'), may hold values from -0.125 to 0.125
- up_weight: bfloat16 [8, 2560, 4096], P('expert', None, 'tensor'), may hold values from -0.125 to 0.125
- down_weight: bfloat16 [8, 4096, 2560], P('expert', 'tensor'), may hold values from -0.09375 to 0.09375
Outputs:
- grad_tokens: bfloat16 [4096, 2560], P(('expert', 'tensor'))
- grad_score: bfloat16 [4096], P(('expert', 'tensor'))
- grad_down_weight: bfloat16 [8, 4096, 2560], P('expert', 'tensor')
The draws below stay inside these ranges and needn't reach their ends.
Inputs may be any that keep to these rules, and one draw needn't show every extreme that they name: `routing`: within the 128 rows of one device no expert is named by more than 20 rows, and in some device's rows one expert is named by exactly 20.
All inputs are finite; a program needn't handle non-finite values.
Results may differ from the reference program's by a relative error of at most 0.014.
Values may be sent and summed in bfloat16 or wider, within the bound.
A program may use at most 192 MiB of HBM per device.

```python
import math
import jax
import jax.numpy as jnp
import numpy as np
from jax import lax

D = 2560
FF = 4096
TOK_DEV = 128
EXPERTS = 8
CAP = 20
SLOTS = 160
GROUP_ROWS = 640
F_DEV = 1024
TOKENS = 4096
N_EXPERT = 8
N_TENSOR = 4


def levels(stream_key, shape, shards, smallest, top_value):
    level, own = 1.0, jax.random.fold_in(stream_key, 6)
    for dim, blocks in shards:
        draws = jnp.exp(jax.random.uniform(jax.random.fold_in(own, dim), (blocks,), jnp.float32, smallest / len(shards), top_value / len(shards)))
        level = level * jnp.repeat(draws, shape[dim] // blocks).reshape([-1 if axis == dim else 1 for axis in range(len(shape))])
    return level


def routed_block(key, own, number, rows, count, top, most, slope):
    order = jax.random.permutation(key, count)
    crowded, ordinary = load_shares(count, rows * top, most, slope, True), load_shares(count, rows * top, most, slope, False)
    places = jnp.arange(count)

    def named(sizes, turn):
        used = int((sizes > 0).sum())
        fixed = max(1, used // 4)
        passed = fixed + (places - fixed + turn * (used - fixed)) % max(1, count - fixed)
        return jnp.zeros((count,), jnp.int32).at[order[jnp.where(places < fixed, places, passed)]].set(jnp.asarray(sizes, jnp.int32))

    sizes = jnp.where(number % 4 == 0, named(crowded, number // 4), named(ordinary, number - number // 4 - 1))
    mixed = jax.random.permutation(jax.random.fold_in(own, 3), count)
    donor, receiver = mixed[0:count // 2 * 2:2], mixed[1:count // 2 * 2:2]
    slack = jnp.minimum(sizes[donor] - 1, most - sizes[receiver]) // 2
    slack = jnp.where((donor == order[0]) | (receiver == order[0]) | (sizes[receiver] == 0), 0, jnp.maximum(slack, 0))
    passed = jax.random.randint(jax.random.fold_in(own, 4), (count // 2,), 0, 1 << 20) % (slack + 1)
    sizes = sizes.at[donor].add(-passed).at[receiver].add(passed)
    members = jnp.searchsorted(jnp.cumsum(sizes), jnp.arange(rows * top), side="right").astype(jnp.int32)
    grid = members.reshape(top, rows).T
    grid = grid[jax.random.permutation(jax.random.fold_in(own, 1), rows)]
    turn = jax.random.randint(jax.random.fold_in(own, 2), (rows, 1), 0, top)
    return jnp.take_along_axis(grid, (jnp.arange(top)[None, :] + turn) % top, axis=1)


def load_shares(number_of, total, reach, slope, full):
    loads = [(1 << 20) // math.isqrt(grade ** slope) + 1 for grade in range(1, number_of + 1)]
    largest = reach if full else min(reach, max(-(-total // number_of), total * loads[0] // sum(loads)))
    least = 1 if total - largest >= number_of - 1 else 0
    counts, rest = [largest] + [least] * (number_of - 1), total - largest - least * (number_of - 1)
    while rest > 0:
        candidates = [i for i in range(1, number_of) if counts[i] < largest] or [i for i in range(1, number_of) if counts[i] < reach]
        pool, remaining = sum([loads[i] for i in candidates]), rest
        for i in candidates:
            extra = min(reach - counts[i], max(1, remaining * loads[i] // pool), rest)
            counts[i] = counts[i] + extra
            rest = rest - extra
    return np.array(counts)


def normal_values(key, extent, width, reach, pieces=(), kind=jnp.bfloat16):
    result = width * jax.random.normal(key, extent, jnp.float32)
    if pieces:
        result = result * levels(key, extent, pieces, -0.22, 0.18)
    return jnp.clip(result, -reach, reach).astype(kind)


def setup_inputs(seed: int = 0) -> dict:
    key_list = jax.random.split(jax.random.key(seed), 9)
    grad_out = normal_values(key_list[0], (TOKENS, D), 1.0, 6.0, ((0, 32),))
    router_score = jnp.clip(0.19921875 + 0.80078125 * jax.random.uniform(key_list[1], (TOKENS,), jnp.float32) ** levels(key_list[1], (TOKENS,), ((0, 32),), -0.2, 0.2), 0.19921875, 1.0).astype(jnp.bfloat16)
    routing_keys = jax.random.split(jax.random.fold_in(key_list[2], 1), TOKENS // TOK_DEV)
    routing_turns = jax.random.permutation(jax.random.fold_in(key_list[2], 3), TOKENS // TOK_DEV)
    routing = jax.vmap(lambda own, number: routed_block(jax.random.fold_in(key_list[2], 2), own, number, TOK_DEV, EXPERTS, 1, CAP, 2))(routing_keys, routing_turns).reshape((TOKENS, 1))
    gate_pre = normal_values(key_list[3], (EXPERTS, GROUP_ROWS, FF), 1.5, 6.0, ((0, 8), (2, 4)))
    up_pre = normal_values(key_list[4], (EXPERTS, GROUP_ROWS, FF), 1.0, 6.0, ((0, 8), (2, 4)))
    gate_weight = normal_values(key_list[5], (EXPERTS, D, FF), D ** -0.5, 0.125, ((0, 8), (2, 4)))
    up_weight = normal_values(key_list[6], (EXPERTS, D, FF), D ** -0.5, 0.125, ((0, 8), (2, 4)))
    down_weight = normal_values(key_list[7], (EXPERTS, FF, D), FF ** -0.5, 0.09375, ((0, 8), (1, 4)))
    return dict(grad_out=grad_out, router_score=router_score, routing=routing, gate_pre=gate_pre, up_pre=up_pre, gate_weight=gate_weight, up_weight=up_weight, down_weight=down_weight)


def expert_backward(inputs):
    rows_grad, rows_score, gate_rows, up_rows, gate_mat, up_mat, down_mat = inputs
    through = jnp.dot(rows_grad, down_mat.T, preferred_element_type=jnp.float32)
    gate_val = gate_rows.astype(jnp.float32)
    up_val = up_rows.astype(jnp.float32)
    sig_gate = jax.nn.sigmoid(gate_val)
    hidden = gate_val * sig_gate * up_val
    slot_score = jnp.sum(through * hidden, axis=1)
    scale_col = rows_score.astype(jnp.float32)[:, None]
    scaled = scale_col * through
    grad_gate = (scaled * up_val * sig_gate * (1.0 + gate_val * (1.0 - sig_gate))).astype(jnp.bfloat16)
    grad_up = (scaled * gate_val * sig_gate).astype(jnp.bfloat16)
    weighted = (scale_col * hidden).astype(jnp.bfloat16)
    grad_down = jnp.dot(weighted.T, rows_grad, preferred_element_type=jnp.float32).astype(jnp.bfloat16)

    def add_block(running, block_index):
        offset = (block_index * F_DEV).astype(jnp.int32)
        gate_cols = lax.dynamic_slice_in_dim(grad_gate, offset, F_DEV, 1)
        up_cols = lax.dynamic_slice_in_dim(grad_up, offset, F_DEV, 1)
        gate_part = lax.dynamic_slice_in_dim(gate_mat, offset, F_DEV, 1)
        up_part = lax.dynamic_slice_in_dim(up_mat, offset, F_DEV, 1)
        term = jnp.dot(gate_cols, gate_part.T, preferred_element_type=jnp.float32)
        term = term + jnp.dot(up_cols, up_part.T, preferred_element_type=jnp.float32)
        rounded = lax.optimization_barrier(term.astype(jnp.bfloat16))
        return running + rounded.astype(jnp.float32), None

    start_sum = jnp.zeros((rows_grad.shape[0], rows_grad.shape[1]), jnp.float32)
    total, unused = lax.scan(add_block, start_sum, jnp.arange(N_TENSOR, dtype=jnp.int32))
    return total.astype(jnp.bfloat16), slot_score, grad_down


def reference(grad_out, router_score, routing, gate_pre, up_pre, gate_weight, up_weight, down_weight):
    expert_ids = routing[:, 0].astype(jnp.int32)
    onehot = (expert_ids[:, None] == jnp.arange(EXPERTS, dtype=jnp.int32)[None, :]).astype(jnp.int32)
    onehot = onehot.reshape(N_EXPERT * N_TENSOR, TOK_DEV, EXPERTS)
    before = jnp.cumsum(onehot, axis=1) - onehot
    position = jnp.sum(before * onehot, axis=2).reshape(TOKENS).astype(jnp.int32)
    device = jnp.arange(TOKENS, dtype=jnp.int32) // TOK_DEV
    slot_row = (device % N_TENSOR) * SLOTS + (device // N_TENSOR) * CAP + position
    group_grad = jnp.zeros((EXPERTS, GROUP_ROWS, D), jnp.bfloat16).at[expert_ids, slot_row].set(grad_out)
    group_score = jnp.zeros((EXPERTS, GROUP_ROWS), jnp.bfloat16).at[expert_ids, slot_row].set(router_score)
    slot_grad, slot_score, grad_down_weight = lax.map(
        expert_backward, (group_grad, group_score, gate_pre, up_pre, gate_weight, up_weight, down_weight))
    grad_tokens = slot_grad[expert_ids, slot_row]
    grad_score = slot_score[expert_ids, slot_row].astype(jnp.bfloat16)
    return grad_tokens, grad_score, grad_down_weight
```

```python
import functools

import jax
import jax.numpy as jnp
from jax import lax
from jax.experimental import pallas as pl
from jax.experimental.pallas import tpu as pltpu
from jax.sharding import PartitionSpec as P

MESH = pl.DeviceIdType.MESH
LANES = 128
PARTS = 4
CHUNK = PARTS * LANES
ROW_TILE = 16
F32 = jnp.float32
BF16 = jnp.bfloat16


def dot_nn(a, b):
    return lax.dot_general(a, b, (((1,), (0,)), ((), ())), preferred_element_type=F32)


def dot_nt(a, b):
    return lax.dot_general(a, b, (((1,), (1,)), ((), ())), preferred_element_type=F32)


def dot_tn(a, b):
    return lax.dot_general(a, b, (((0,), (0,)), ((), ())), preferred_element_type=F32)


def split_bf16(value):
    high = value.astype(BF16)
    return high, (value - high.astype(F32)).astype(BF16)


def iota(shape, dim):
    return lax.broadcasted_iota(jnp.int32, shape, dim)


def one_where(mask):
    return jnp.where(mask, 1.0, 0.0).astype(BF16)


def kernel(
    n_expert, cap, n_chunk,
    grad_ref, score_ref, routing_ref, gate_pre_ref, up_pre_ref, gate_w_ref, up_w_ref, down_w_ref,
    tokens_ref, score_out_ref, down_out_ref,
    gate_w, up_w, down_w, gate_v, up_v, coef_gate, coef_up, hidden, through, grad_gate, grad_up,
    pick_send, pick_back, gather_mat, spread_mat,
    send, recv, rows, term, got_first, sum_out, got_second, ret, back, down_part,
    row_sum, score_part, score_got, score_tot, score_back,
    z_send, z_recv, ag_send, ag_recv, first_send, first_recv, second_send, second_recv,
    rz_send, rz_recv, sp_send, sp_recv, sz_send, sz_recv, load_sem, out_sem,
):
    tok = grad_ref.shape[0]
    block = n_expert * cap
    half = block // 2
    piece = PARTS * cap
    n_rows = PARTS * block
    hid = gate_v.shape[1]
    me_e = lax.axis_index("expert")
    me_t = lax.axis_index("tensor")
    tx = me_t + 1 - 2 * lax.rem(me_t, 2)
    ty = lax.rem(me_t + 2, 4)
    td = 3 - me_t
    peers = (me_t, tx, ty, td)

    barrier = pltpu.get_barrier_semaphore()
    for d in range(1, n_expert):
        pl.semaphore_signal(
            barrier, inc=1, device_id=(lax.rem(me_e + d, n_expert), me_t), device_id_type=MESH
        )
    for j in range(1, 4):
        pl.semaphore_signal(barrier, inc=1, device_id=(me_e, peers[j]), device_id_type=MESH)

    loads = []
    for j in range(4):
        start = pl.multiple_of(peers[j] * block, block)
        for k, (src, dst) in enumerate(((gate_pre_ref, gate_v), (up_pre_ref, up_v))):
            loads.append(
                pltpu.make_async_copy(
                    src.at[0, pl.ds(start, block)],
                    dst.at[pl.ds(j * block, block)],
                    load_sem.at[2 * j + k],
                )
            )
    load_down = pltpu.make_async_copy(down_w_ref.at[0], down_w, load_sem.at[8])
    load_gate = pltpu.make_async_copy(gate_w_ref.at[0], gate_w, load_sem.at[9])
    load_up = pltpu.make_async_copy(up_w_ref.at[0], up_w, load_sem.at[10])
    for copy in loads + [load_down, load_gate, load_up]:
        copy.start()

    def remote(src, dst, s_sem, r_sem, e, t):
        return pltpu.make_async_remote_copy(
            src_ref=src, dst_ref=dst, send_sem=s_sem, recv_sem=r_sem,
            device_id=(e, t), device_id_type=MESH,
        )

    routing = routing_ref[...]
    named = iota((ROW_TILE, tok), 0) == routing
    earlier = one_where(iota((tok, tok), 0) < iota((tok, tok), 1))
    before = dot_nn(one_where(named), earlier)
    place = jnp.sum(jnp.where(named, before, 0.0), axis=0, keepdims=True).astype(jnp.int32)
    key = routing * piece + place
    score = score_ref[...].astype(F32)
    spot = iota((n_expert * piece, tok), 0)
    for q in range(PARTS):
        pick_send[:, q * tok : (q + 1) * tok] = jnp.where(
            spot == key + q * cap, score, 0.0
        ).astype(BF16)

    def z_copy(c, d):
        dest = lax.rem(me_e + d, n_expert)
        return remote(
            send.at[c, dest], recv.at[c, me_e], z_send.at[c, d], z_recv.at[c, d], dest, me_t
        )

    far_first = sorted(range(1, n_expert), key=lambda d: -min(d, n_expert - d))

    for c in range(n_chunk):
        stack = jnp.concatenate(
            [
                grad_ref[:, c * CHUNK + q * LANES : c * CHUNK + (q + 1) * LANES]
                for q in range(PARTS)
            ],
            axis=0,
        )
        out = dot_nn(pick_send[...], stack).astype(BF16)
        send[c] = out.reshape(n_expert, piece, LANES)
        if c == 0:
            pl.semaphore_wait(barrier, n_expert - 1 + 3)
        for d in far_first:
            z_copy(c, d).start()
        recv[c, me_e] = send[c, me_e]

    for q in range(PARTS):
        r = iota((block, n_expert * piece), 0)
        s = sum((r >= k * cap).astype(jnp.int32) for k in range(1, n_expert))
        gather_mat[q * block : (q + 1) * block, :] = one_where(
            iota((block, n_expert * piece), 1) == r + s * (piece - cap) + q * cap
        )

    def ag_copy(c, k):
        if k == 0:
            src, dst, t = rows.at[c, 0:block], rows.at[c, block : 2 * block], tx
        elif k == 1:
            src, dst, t = rows.at[c, 0:block], rows.at[c, 2 * block : 3 * block], ty
        elif k == 2:
            src, dst, t = (
                rows.at[c, block : block + half], rows.at[c, 3 * block : 3 * block + half], ty
            )
        else:
            src, dst, t = (
                rows.at[c, 2 * block + half : 3 * block],
                rows.at[c, 3 * block + half : 4 * block],
                tx,
            )
        return remote(src, dst, ag_send.at[c, k], ag_recv.at[c, k], me_e, t)

    def arrive(c):
        for d in far_first[::-1]:
            z_copy(c, d).wait_recv()
        pieces = recv[c].reshape(n_expert * piece, LANES)
        out = dot_nn(gather_mat[...], pieces).astype(BF16)
        for q in range(PARTS):
            rows[c, 0:block, q * LANES : (q + 1) * LANES] = out[q * block : (q + 1) * block]
        ag_copy(c, 0).start()
        ag_copy(c, 1).start()

    def forward(c):
        ag_copy(c, 0).wait_recv()
        ag_copy(c, 2).start()
        ag_copy(c, 1).wait_recv()
        ag_copy(c, 3).start()

    def through_part(c):
        ag_copy(c, 2).wait_recv()
        ag_copy(c, 3).wait_recv()

        def body(j, carry):
            at = pl.ds(pl.multiple_of(j * block, block), block)
            part = dot_nt(rows[c, at, :], down_w[:, c * CHUNK : (c + 1) * CHUNK])
            if c == 0:
                through[at, :] = part
            else:
                through[at, :] = through[at, :] + part
            return carry

        lax.fori_loop(0, 4, body, 0)

    def down_copy(c):
        return pltpu.make_async_copy(
            down_part.at[c], down_out_ref.at[0, :, c * CHUNK : (c + 1) * CHUNK], out_sem.at[c]
        )

    def down_term(c):
        def body(i, carry):
            at = pl.ds(pl.multiple_of(i * 256, 256), 256)
            down_part[c, at, :] = dot_tn(hidden[:, at], rows[c]).astype(BF16)
            return carry

        lax.fori_loop(0, hid // 256, body, 0)
        down_copy(c).start()

    def coefficients():
        for copy in loads:
            copy.wait()

        def body(i, carry):
            at = pl.ds(pl.multiple_of(i * ROW_TILE, ROW_TILE), ROW_TILE)
            gate = gate_v[at, :].astype(F32)
            up = up_v[at, :].astype(F32)
            sig = lax.logistic(gate)
            silu = gate * sig
            coef_up[at, :] = silu
            coef_gate[at, :] = up * sig * (1.0 + gate * (1.0 - sig))
            hidden[at, :] = (silu * up).astype(BF16)
            return carry

        lax.fori_loop(0, n_rows // ROW_TILE, body, 0)

    arrive(0)
    arrive(1)
    coefficients()
    forward(0)
    arrive(2)
    load_down.wait()
    forward(1)
    through_part(0)
    arrive(3)
    forward(2)
    through_part(1)
    arrive(4)
    forward(3)
    y = iota((n_expert * piece, PARTS * block), 1)
    q_of = sum((y >= k * block).astype(jnp.int32) for k in range(1, PARTS))
    r_of = y - q_of * block
    s_of = sum((r_of >= k * cap).astype(jnp.int32) for k in range(1, n_expert))
    spread_mat[...] = one_where(
        iota((n_expert * piece, PARTS * block), 0) == r_of + s_of * (piece - cap) + q_of * cap
    )
    key_f = key.astype(F32)
    key_col = jnp.sum(
        jnp.where(iota((tok, tok), 0) == iota((tok, tok), 1), key_f, 0.0), axis=1, keepdims=True
    ).astype(jnp.int32)
    lane_spot = iota((tok, n_expert * piece), 1)
    for q in range(PARTS):
        pick_back[q * tok : (q + 1) * tok, :] = one_where(lane_spot == key_col + q * cap)
    through_part(2)
    forward(4)
    down_term(0)
    through_part(3)
    down_term(1)
    load_gate.wait()
    load_up.wait()
    through_part(4)

    def grads(i, carry):
        at = pl.ds(pl.multiple_of(i * ROW_TILE, ROW_TILE), ROW_TILE)
        value = through[at, :]
        silu = coef_up[at, :]
        grad_gate[at, :] = (value * coef_gate[at, :]).astype(BF16)
        grad_up[at, :] = (value * silu).astype(BF16)
        prod = value * silu * up_v[at, :].astype(F32)
        total = prod[:, 0:LANES]
        for k in range(1, hid // LANES):
            total = total + prod[:, k * LANES : (k + 1) * LANES]
        row_sum[at, :] = total
        return carry

    lax.fori_loop(0, n_rows // ROW_TILE, grads, 0)

    def first_copy(c, k):
        begin = ((block, tx), (3 * block, tx), (2 * block + half, ty), (3 * block + half, ty))[k]
        return remote(
            term.at[c, begin[0] : begin[0] + half], got_first.at[c, k],
            first_send.at[c, k], first_recv.at[c, k], me_e, begin[1],
        )

    def second_copy(c, k):
        return remote(
            sum_out.at[c, k], got_second.at[c, k],
            second_send.at[c, k], second_recv.at[c, k], me_e, (ty, tx)[k],
        )

    def rz_copy(c, d):
        dest = lax.rem(me_e + d, n_expert)
        return remote(
            ret.at[c, dest], back.at[c, me_e], rz_send.at[c, d], rz_recv.at[c, d], dest, me_t
        )

    def make_term(c):
        gate_c = gate_w.at[c * CHUNK : (c + 1) * CHUNK, :]
        up_c = up_w.at[c * CHUNK : (c + 1) * CHUNK, :]

        def body(j, carry):
            at = pl.ds(pl.multiple_of(j * block, block), block)
            value = dot_nt(grad_gate[at, :], gate_c[...]) + dot_nt(grad_up[at, :], up_c[...])
            term[c, at, :] = value.astype(BF16)
            return carry

        lax.fori_loop(0, 4, body, 0)
        for k in range(4):
            first_copy(c, k).start()

    def add(a, b):
        return a.astype(F32) + b.astype(F32)

    def second_stage(c):
        for k in range(2):
            first_copy(c, k).wait_recv()
        sum_out[c, 0] = add(term[c, 2 * block : 2 * block + half], got_first[c, 1]).astype(BF16)
        second_copy(c, 0).start()
        for k in range(2, 4):
            first_copy(c, k).wait_recv()
        sum_out[c, 1] = add(term[c, block + half : 2 * block], got_first[c, 3]).astype(BF16)
        second_copy(c, 1).start()

    def send_home(c):
        second_copy(c, 0).wait_recv()
        second_copy(c, 1).wait_recv()
        low = add(term[c, 0:half], got_first[c, 0]) + got_second[c, 0].astype(F32)
        high = add(term[c, half:block], got_first[c, 2]) + got_second[c, 1].astype(F32)
        total = jnp.concatenate([low.astype(BF16), high.astype(BF16)], axis=0)
        stack = jnp.concatenate(
            [total[:, q * LANES : (q + 1) * LANES] for q in range(PARTS)], axis=0
        )
        out = dot_nn(spread_mat[...], stack).astype(BF16)
        ret[c] = out.reshape(n_expert, piece, LANES)
        for d in far_first:
            rz_copy(c, d).start()
        back[c, me_e] = ret[c, me_e]

    def finish(c):
        for d in far_first[::-1]:
            rz_copy(c, d).wait_recv()
        out = dot_nn(pick_back[...], back[c].reshape(n_expert * piece, LANES)).astype(BF16)
        for q in range(PARTS):
            tokens_ref[:, c * CHUNK + q * LANES : c * CHUNK + (q + 1) * LANES] = out[
                q * tok : (q + 1) * tok
            ]

    wide = score_part.shape[2]

    def sp_copy(j):
        return remote(
            score_part.at[j], score_got.at[j], sp_send.at[j], sp_recv.at[j], me_e, peers[j]
        )

    def sz_copy(d):
        dest = lax.rem(me_e + d, n_expert)
        return remote(
            score_tot, score_back.at[me_e], sz_send.at[d], sz_recv.at[d], dest, me_t
        )

    def send_scores():
        ones = jnp.ones((ROW_TILE, LANES), BF16)
        score_part[...] = jnp.zeros(score_part.shape, F32)
        for j in range(4):
            high, low = split_bf16(row_sum[j * block : (j + 1) * block, :])
            line = dot_nt(ones, high) + dot_nt(ones, low)
            score_part[j, :, 0:block] = line[0:8]
        for j in range(1, 4):
            sp_copy(j).start()

    def total_scores():
        for j in range(1, 4):
            sp_copy(j).wait_recv()
        score_tot[...] = (score_part[0] + score_got[1]) + (score_got[2] + score_got[3])
        for d in far_first:
            sz_copy(d).start()
        score_back[me_e] = score_tot[...]

    def finish_scores():
        for d in far_first:
            sz_copy(d).wait_recv()
        lane = iota((wide, tok), 0)
        pick = one_where(lane == me_e * cap + place)
        high, low = split_bf16(score_back[...].reshape(n_expert * 8, wide))
        mixed = dot_nn(high, pick) + dot_nn(low, pick)
        keep = iota((n_expert * 8, tok), 0) == routing * 8
        value = jnp.sum(jnp.where(keep, mixed, 0.0), axis=0, keepdims=True)
        score_out_ref[...] = (value / score).astype(BF16)

    make_term(0)
    make_term(1)
    send_scores()
    second_stage(0)
    make_term(2)
    second_stage(1)
    send_home(0)
    down_term(2)
    make_term(3)
    second_stage(2)
    send_home(1)
    total_scores()
    make_term(4)
    second_stage(3)
    send_home(2)
    finish(0)
    down_term(3)
    second_stage(4)
    send_home(3)
    finish(1)
    down_term(4)
    send_home(4)
    finish(2)
    finish_scores()
    finish(3)
    finish(4)

    for c in range(n_chunk):
        for d in range(1, n_expert):
            z_copy(c, d).wait_send()
            rz_copy(c, d).wait_send()
        for k in range(4):
            ag_copy(c, k).wait_send()
            first_copy(c, k).wait_send()
        for k in range(2):
            second_copy(c, k).wait_send()
        down_copy(c).wait()
    for j in range(1, 4):
        sp_copy(j).wait_send()
    for d in range(1, n_expert):
        sz_copy(d).wait_send()


def fused_local(grad_out, router_score, routing, gate_pre, up_pre, gate_weight, up_weight, down_weight):
    n_expert = lax.axis_size("expert")
    tok, width = grad_out.shape
    cap = tok // n_expert + tok // (4 * n_expert)
    block = n_expert * cap
    piece = PARTS * cap
    n_rows = gate_pre.shape[1]
    hid = gate_pre.shape[2]
    n_chunk = width // CHUNK
    wide = -(-block // LANES) * LANES
    vmem = pl.BlockSpec(memory_space=pltpu.VMEM)
    hbm = pl.BlockSpec(memory_space=pl.ANY)
    dma = pltpu.SemaphoreType.DMA
    macs = 4 * n_rows * width * hid
    tokens, score, down = pl.pallas_call(
        functools.partial(kernel, n_expert, cap, n_chunk),
        out_shape=(
            jax.ShapeDtypeStruct((tok, width), BF16),
            jax.ShapeDtypeStruct((1, tok), BF16),
            jax.ShapeDtypeStruct((1, hid, width), BF16),
        ),
        in_specs=[vmem, vmem, vmem, hbm, hbm, hbm, hbm, hbm],
        out_specs=(vmem, vmem, hbm),
        scratch_shapes=[
            pltpu.VMEM((width, hid), BF16),
            pltpu.VMEM((width, hid), BF16),
            pltpu.VMEM((hid, width), BF16),
            pltpu.VMEM((n_rows, hid), BF16),
            pltpu.VMEM((n_rows, hid), BF16),
            pltpu.VMEM((n_rows, hid), F32),
            pltpu.VMEM((n_rows, hid), F32),
            pltpu.VMEM((n_rows, hid), BF16),
            pltpu.VMEM((n_rows, hid), F32),
            pltpu.VMEM((n_rows, hid), BF16),
            pltpu.VMEM((n_rows, hid), BF16),
            pltpu.VMEM((n_expert * piece, PARTS * tok), BF16),
            pltpu.VMEM((PARTS * tok, n_expert * piece), BF16),
            pltpu.VMEM((PARTS * block, n_expert * piece), BF16),
            pltpu.VMEM((n_expert * piece, PARTS * block), BF16),
            pltpu.VMEM((n_chunk, n_expert, piece, LANES), BF16),
            pltpu.VMEM((n_chunk, n_expert, piece, LANES), BF16),
            pltpu.VMEM((n_chunk, n_rows, CHUNK), BF16),
            pltpu.VMEM((n_chunk, n_rows, CHUNK), BF16),
            pltpu.VMEM((n_chunk, 4, block // 2, CHUNK), BF16),
            pltpu.VMEM((n_chunk, 2, block // 2, CHUNK), BF16),
            pltpu.VMEM((n_chunk, 2, block // 2, CHUNK), BF16),
            pltpu.VMEM((n_chunk, n_expert, piece, LANES), BF16),
            pltpu.VMEM((n_chunk, n_expert, piece, LANES), BF16),
            pltpu.VMEM((n_chunk, hid, CHUNK), BF16),
            pltpu.VMEM((n_rows, LANES), F32),
            pltpu.VMEM((4, 8, wide), F32),
            pltpu.VMEM((4, 8, wide), F32),
            pltpu.VMEM((8, wide), F32),
            pltpu.VMEM((n_expert, 8, wide), F32),
            dma((n_chunk, n_expert)),
            dma((n_chunk, n_expert)),
            dma((n_chunk, 4)),
            dma((n_chunk, 4)),
            dma((n_chunk, 4)),
            dma((n_chunk, 4)),
            dma((n_chunk, 2)),
            dma((n_chunk, 2)),
            dma((n_chunk, n_expert)),
            dma((n_chunk, n_expert)),
            dma((4,)),
            dma((4,)),
            dma((n_expert,)),
            dma((n_expert,)),
            dma((11,)),
            dma((n_chunk,)),
        ],
        compiler_params=pltpu.CompilerParams(
            collective_id=0, has_side_effects=True, vmem_limit_bytes=60 * 1024 * 1024
        ),
        cost_estimate=pl.CostEstimate(
            flops=2 * macs,
            bytes_accessed=2 * (4 * width * hid + 2 * n_rows * hid),
            transcendentals=n_rows * hid,
        ),
        name="routed_backward",
    )(
        grad_out,
        router_score.reshape(1, tok),
        routing.reshape(1, tok),
        gate_pre,
        up_pre,
        gate_weight,
        up_weight,
        down_weight,
    )
    return tokens, score.reshape(tok), down


def fits(mesh, grad_out, gate_pre):
    n_expert, n_tensor = mesh.shape["expert"], mesh.shape["tensor"]
    tok = grad_out.shape[0] // (n_expert * n_tensor)
    cap = tok // n_expert + tok // (4 * n_expert)
    return (
        n_tensor == 4
        and n_expert <= ROW_TILE
        and cap % 4 == 0
        and (n_expert * cap) % 32 == 0
        and tok % LANES == 0
        and grad_out.shape[1] == 5 * CHUNK
        and gate_pre.shape[2] % (256 * n_tensor) == 0
    )


def expert_rows(rows_grad, rows_score, gate_rows, up_rows, down_local):
    through = lax.dot_general(
        rows_grad, down_local, (((1,), (1,)), ((), ())), preferred_element_type=jnp.float32
    )
    gate_val = gate_rows.astype(jnp.float32)
    up_val = up_rows.astype(jnp.float32)
    sig_gate = jax.nn.sigmoid(gate_val)
    hidden = gate_val * sig_gate * up_val
    part_score = jnp.sum(through * hidden, axis=1)
    scale_col = rows_score.astype(jnp.float32)[:, None]
    scaled = scale_col * through
    grad_gate = (scaled * up_val * sig_gate * (1.0 + gate_val * (1.0 - sig_gate))).astype(
        jnp.bfloat16
    )
    grad_up = (scaled * gate_val * sig_gate).astype(jnp.bfloat16)
    weighted = (scale_col * hidden).astype(jnp.bfloat16)
    down_term = lax.dot_general(
        weighted, rows_grad, (((0,), (0,)), ((), ())), preferred_element_type=jnp.float32
    )
    return (grad_gate, grad_up, part_score, down_term)


def local(grad_out, router_score, routing, gate_pre, up_pre, gate_weight, up_weight, down_weight):
    n_expert = lax.axis_size("expert")
    tok_count = grad_out.shape[0]
    width = grad_out.shape[1]
    capacity = tok_count // n_expert + tok_count // (4 * n_expert)
    slot_count = n_expert * capacity
    gate_local = gate_pre[0]
    up_local = up_pre[0]
    down_local = down_weight[0]
    gate_mat = gate_weight[0]
    up_mat = up_weight[0]
    expert_ids = routing[:, 0]
    onehot = (expert_ids[:, None] == jnp.arange(n_expert, dtype=jnp.int32)[None, :]).astype(
        jnp.int32
    )
    before = jnp.cumsum(onehot, axis=0) - onehot
    position = jnp.sum(before * onehot, axis=1)
    slot_index = expert_ids * capacity + position
    send_grad = jnp.zeros((slot_count, width), jnp.bfloat16).at[slot_index].set(grad_out)
    send_score = jnp.zeros((slot_count,), jnp.bfloat16).at[slot_index].set(router_score)
    recv_grad, recv_score = (
        lax.all_to_all(
            send_grad.reshape(n_expert, capacity, width),
            "expert",
            split_axis=0,
            concat_axis=0,
            tiled=True,
        ),
        lax.all_to_all(
            send_score.reshape(n_expert, capacity),
            "expert",
            split_axis=0,
            concat_axis=0,
            tiled=True,
        ),
    )
    recv_grad = recv_grad.reshape(slot_count, width)
    recv_score = recv_score.reshape(slot_count)
    all_grad, all_score = (
        lax.all_gather(recv_grad, "tensor", axis=0, tiled=True),
        lax.all_gather(recv_score, "tensor", axis=0, tiled=True),
    )
    grad_gate, grad_up, part_score, down_sum = expert_rows(
        all_grad, all_score, gate_local, up_local, down_local
    )
    term = lax.dot_general(
        grad_gate, gate_mat, (((1,), (1,)), ((), ())), preferred_element_type=jnp.float32
    )
    mine_grad = lax.psum_scatter(
        (
            term
            + lax.dot_general(
                grad_up, up_mat, (((1,), (1,)), ((), ())), preferred_element_type=jnp.float32
            )
        ).astype(jnp.bfloat16),
        "tensor",
        scatter_dimension=0,
        tiled=True,
    )
    mine_score = lax.psum_scatter(part_score, "tensor", scatter_dimension=0, tiled=True)
    back_grad, back_score = (
        lax.all_to_all(
            mine_grad.reshape(n_expert, capacity, width),
            "expert",
            split_axis=0,
            concat_axis=0,
            tiled=True,
        ),
        lax.all_to_all(
            mine_score.astype(jnp.bfloat16).reshape(n_expert, capacity),
            "expert",
            split_axis=0,
            concat_axis=0,
            tiled=True,
        ),
    )
    grad_tokens = back_grad.reshape(slot_count, width)[slot_index]
    grad_score = back_score.reshape(slot_count)[slot_index]
    grad_down_weight = down_sum.astype(jnp.bfloat16)[None]
    return (grad_tokens, grad_score, grad_down_weight)


def solution(mesh):
    def run(*arrays):
        body = fused_local if fits(mesh, arrays[0], arrays[3]) else local
        return jax.shard_map(
            body,
            mesh=mesh,
            in_specs=(
                P(("expert", "tensor"), None),
                P(("expert", "tensor")),
                P(("expert", "tensor"), None),
                P("expert", None, "tensor"),
                P("expert", None, "tensor"),
                P("expert", None, "tensor"),
                P("expert", None, "tensor"),
                P("expert", "tensor", None),
            ),
            out_specs=(
                P(("expert", "tensor"), None),
                P(("expert", "tensor")),
                P("expert", "tensor", None),
            ),
            check_vma=False,
        )(*arrays)

    return run
```

```python
import functools

import jax
import jax.numpy as jnp
from jax import lax
from jax.experimental import pallas as pl
from jax.experimental.pallas import tpu as pltpu
from jax.sharding import PartitionSpec as P

MESH = pl.DeviceIdType.MESH
LANES = 128
PARTS = 4
CHUNK = PARTS * LANES
ROW_TILE = 16
TILE = 256
F32 = jnp.float32
BF16 = jnp.bfloat16


def dot_nn(a, b):
    return lax.dot_general(a, b, (((1,), (0,)), ((), ())), preferred_element_type=F32)


def dot_nt(a, b):
    return lax.dot_general(a, b, (((1,), (1,)), ((), ())), preferred_element_type=F32)


def dot_tn(a, b):
    return lax.dot_general(a, b, (((0,), (0,)), ((), ())), preferred_element_type=F32)


def split_bf16(value):
    high = value.astype(BF16)
    return high, (value - high.astype(F32)).astype(BF16)


def iota(shape, dim):
    return lax.broadcasted_iota(jnp.int32, shape, dim)


def one_where(mask):
    return jnp.where(mask, 1.0, 0.0).astype(BF16)


def kernel(
    n_expert, cap, n_chunk,
    grad_ref, score_ref, routing_ref, gate_pre_ref, up_pre_ref, gate_w_ref, up_w_ref, down_w_ref,
    tokens_ref, score_out_ref, down_out_ref,
    gate_w, up_w, down_w, gate_v, up_v, coef_gate, coef_up, hidden_t, through, grad_gate, grad_up,
    pick_send, pick_back, gather_mat, spread_mat,
    send, recv, rows, term, got_first, sum_out, got_second, ret, back,
    row_sum, score_part, score_got, score_tot, score_back,
    z_send, z_recv, ag_send, ag_recv, first_send, first_recv, second_send, second_recv,
    rz_send, rz_recv, sp_send, sp_recv, sz_send, sz_recv, load_sem,
):
    tok = grad_ref.shape[0]
    block = n_expert * cap
    half = block // 2
    piece = PARTS * cap
    n_rows = PARTS * block
    hid = gate_v.shape[1]
    me_e = lax.axis_index("expert")
    me_t = lax.axis_index("tensor")
    tx = me_t + 1 - 2 * lax.rem(me_t, 2)
    ty = lax.rem(me_t + 2, 4)
    td = 3 - me_t
    peers = (me_t, tx, ty, td)

    barrier = pltpu.get_barrier_semaphore()
    for d in range(1, n_expert):
        pl.semaphore_signal(
            barrier, inc=1, device_id=(lax.rem(me_e + d, n_expert), me_t), device_id_type=MESH
        )
    for j in range(1, 4):
        pl.semaphore_signal(barrier, inc=1, device_id=(me_e, peers[j]), device_id_type=MESH)

    loads = []
    for j in range(4):
        start = pl.multiple_of(peers[j] * block, block)
        for k, (src, dst) in enumerate(((gate_pre_ref, gate_v), (up_pre_ref, up_v))):
            loads.append(
                pltpu.make_async_copy(
                    src.at[0, pl.ds(start, block)],
                    dst.at[pl.ds(j * block, block)],
                    load_sem.at[2 * j + k],
                )
            )
    load_down = pltpu.make_async_copy(down_w_ref.at[0], down_w, load_sem.at[8])
    load_gate = pltpu.make_async_copy(gate_w_ref.at[0], gate_w, load_sem.at[9])
    load_up = pltpu.make_async_copy(up_w_ref.at[0], up_w, load_sem.at[10])
    for copy in loads + [load_down, load_gate, load_up]:
        copy.start()

    def remote(src, dst, s_sem, r_sem, e, t):
        return pltpu.make_async_remote_copy(
            src_ref=src, dst_ref=dst, send_sem=s_sem, recv_sem=r_sem,
            device_id=(e, t), device_id_type=MESH,
        )

    routing = routing_ref[...]
    named = iota((ROW_TILE, tok), 0) == routing
    earlier = one_where(iota((tok, tok), 0) < iota((tok, tok), 1))
    before = dot_nn(one_where(named), earlier)
    place = jnp.sum(jnp.where(named, before, 0.0), axis=0, keepdims=True).astype(jnp.int32)
    key = routing * piece + place
    score = score_ref[...].astype(F32)
    spot = iota((n_expert * piece, tok), 0)
    for q in range(PARTS):
        pick_send[:, q * tok : (q + 1) * tok] = jnp.where(
            spot == key + q * cap, score, 0.0
        ).astype(BF16)

    def z_copy(c, d):
        dest = lax.rem(me_e + d, n_expert)
        return remote(
            send.at[c, dest], recv.at[c, me_e], z_send.at[c, d], z_recv.at[c, d], dest, me_t
        )

    far_first = sorted(range(1, n_expert), key=lambda d: -min(d, n_expert - d))

    for c in range(n_chunk):
        stack = jnp.concatenate(
            [
                grad_ref[:, c * CHUNK + q * LANES : c * CHUNK + (q + 1) * LANES]
                for q in range(PARTS)
            ],
            axis=0,
        )
        out = dot_nn(pick_send[...], stack).astype(BF16)
        send[c] = out.reshape(n_expert, piece, LANES)
        if c == 0:
            pl.semaphore_wait(barrier, n_expert - 1 + 3)
        for d in far_first:
            z_copy(c, d).start()
        recv[c, me_e] = send[c, me_e]

    key_f = key.astype(F32)
    key_col = jnp.sum(
        jnp.where(iota((tok, tok), 0) == iota((tok, tok), 1), key_f, 0.0), axis=1, keepdims=True
    ).astype(jnp.int32)
    lane_spot = iota((tok, n_expert * piece), 1)
    for q in range(PARTS):
        pick_back[q * tok : (q + 1) * tok, :] = one_where(lane_spot == key_col + q * cap)
    for q in range(PARTS):
        r = iota((block, n_expert * piece), 0)
        s = sum((r >= k * cap).astype(jnp.int32) for k in range(1, n_expert))
        gather_mat[q * block : (q + 1) * block, :] = one_where(
            iota((block, n_expert * piece), 1) == r + s * (piece - cap) + q * cap
        )
    spread_mat[...] = gather_mat[...].T

    def ag_copy(c, k):
        if k == 0:
            src, dst, t = rows.at[c, 0:block], rows.at[c, block : 2 * block], tx
        elif k == 1:
            src, dst, t = rows.at[c, 0:block], rows.at[c, 2 * block : 3 * block], ty
        elif k == 2:
            src, dst, t = (
                rows.at[c, block : block + half], rows.at[c, 3 * block : 3 * block + half], ty
            )
        else:
            src, dst, t = (
                rows.at[c, 2 * block + half : 3 * block],
                rows.at[c, 3 * block + half : 4 * block],
                tx,
            )
        return remote(src, dst, ag_send.at[c, k], ag_recv.at[c, k], me_e, t)

    def arrive(c):
        for d in far_first[::-1]:
            z_copy(c, d).wait_recv()
        pieces = recv[c].reshape(n_expert * piece, LANES)
        out = dot_nn(gather_mat[...], pieces).astype(BF16)
        for q in range(PARTS):
            rows[c, 0:block, q * LANES : (q + 1) * LANES] = out[q * block : (q + 1) * block]
        ag_copy(c, 0).start()
        ag_copy(c, 1).start()

    def forward(c):
        ag_copy(c, 0).wait_recv()
        ag_copy(c, 2).start()
        ag_copy(c, 1).wait_recv()
        ag_copy(c, 3).start()

    def wait_diagonal(c):
        ag_copy(c, 2).wait_recv()
        ag_copy(c, 3).wait_recv()

    def through_part(c):
        wait_diagonal(c)

        def body(i, carry):
            at = pl.ds(pl.multiple_of(i * TILE, TILE), TILE)
            part = dot_nt(rows[c], down_w[at, c * CHUNK : (c + 1) * CHUNK])
            if c == 0:
                through[:, at] = part
            else:
                through[:, at] = through[:, at] + part
            return carry

        lax.fori_loop(0, hid // TILE, body, 0)

    def down_term(c):
        def body(i, carry):
            at = pl.ds(pl.multiple_of(i * TILE, TILE), TILE)
            to = pl.ds(pl.multiple_of(c * CHUNK + i * TILE, TILE), TILE)
            down_out_ref[0, :, to] = dot_nn(hidden_t[...], rows[c, :, at]).astype(BF16)
            return carry

        lax.fori_loop(0, CHUNK // TILE, body, 0)

    def coefficients():
        for copy in loads:
            copy.wait()

        def body(i, carry):
            at = pl.ds(pl.multiple_of(i * ROW_TILE, ROW_TILE), ROW_TILE)
            gate = gate_v[at, :].astype(F32)
            up = up_v[at, :].astype(F32)
            sig = lax.logistic(gate)
            silu = gate * sig
            coef_up[at, :] = silu
            coef_gate[at, :] = up * sig * (1.0 + gate * (1.0 - sig))
            grad_up[at, :] = (silu * up).astype(BF16)
            return carry

        lax.fori_loop(0, n_rows // ROW_TILE, body, 0)

        def turn(i, carry):
            at = pl.ds(pl.multiple_of(i * LANES, LANES), LANES)
            hidden_t[:, at] = grad_up[at, :].T
            return carry

        lax.fori_loop(0, n_rows // LANES, turn, 0)

    arrive(0)
    arrive(1)
    coefficients()
    forward(0)
    arrive(2)
    load_down.wait()
    forward(1)
    through_part(0)
    arrive(3)
    forward(2)
    through_part(1)
    arrive(4)
    forward(3)
    through_part(2)
    load_gate.wait()
    load_up.wait()
    through_part(3)

    def grads(i, carry):
        at = pl.ds(pl.multiple_of(i * ROW_TILE, ROW_TILE), ROW_TILE)
        value = through[at, :]
        silu = coef_up[at, :]
        grad_gate[at, :] = (value * coef_gate[at, :]).astype(BF16)
        grad_up[at, :] = (value * silu).astype(BF16)
        prod = value * silu * up_v[at, :].astype(F32)
        total = prod[:, 0:LANES]
        for k in range(1, hid // LANES):
            total = total + prod[:, k * LANES : (k + 1) * LANES]
        row_sum[at, :] = total
        return carry

    def finish_block(j):
        last = n_chunk - 1
        span = slice(j * block, (j + 1) * block)

        def body(i, carry):
            at = pl.ds(pl.multiple_of(i * TILE, TILE), TILE)
            part = dot_nt(rows[last, span, :], down_w[at, last * CHUNK : (last + 1) * CHUNK])
            through[span, at] = through[span, at] + part
            return carry

        lax.fori_loop(0, hid // TILE, body, 0)
        per = block // ROW_TILE
        lax.fori_loop(j * per, (j + 1) * per, grads, 0)

    def first_copy(c, k):
        begin = ((block, tx), (3 * block, tx), (2 * block + half, ty), (3 * block + half, ty))[k]
        return remote(
            term.at[c, begin[0] : begin[0] + half], got_first.at[c, k],
            first_send.at[c, k], first_recv.at[c, k], me_e, begin[1],
        )

    def second_copy(c, k):
        return remote(
            sum_out.at[c, k], got_second.at[c, k],
            second_send.at[c, k], second_recv.at[c, k], me_e, (ty, tx)[k],
        )

    def rz_copy(c, d):
        dest = lax.rem(me_e + d, n_expert)
        return remote(
            ret.at[c, dest], back.at[c, me_e], rz_send.at[c, d], rz_recv.at[c, d], dest, me_t
        )

    def make_term(c):
        for n in range(CHUNK // TILE):
            at = slice(c * CHUNK + n * TILE, c * CHUNK + (n + 1) * TILE)

            def body(j, carry):
                span = pl.ds(pl.multiple_of(j * 2 * block, 2 * block), 2 * block)
                value = dot_nt(grad_gate[span, :], gate_w[at, :])
                value = value + dot_nt(grad_up[span, :], up_w[at, :])
                term[c, span, n * TILE : (n + 1) * TILE] = value.astype(BF16)
                return carry

            lax.fori_loop(0, 2, body, 0)
        for k in range(4):
            first_copy(c, k).start()

    def first_block(j):
        span = slice(j * block, (j + 1) * block)

        def body(i, carry):
            at = pl.ds(pl.multiple_of(i * TILE, TILE), TILE)
            value = dot_nt(grad_gate[span, :], gate_w[at, :])
            value = value + dot_nt(grad_up[span, :], up_w[at, :])
            term[0, span, at] = value.astype(BF16)
            return carry

        lax.fori_loop(0, CHUNK // TILE, body, 0)

    def add(a, b):
        return a.astype(F32) + b.astype(F32)

    def second_stage(c):
        for k in range(2):
            first_copy(c, k).wait_recv()
        sum_out[c, 0] = add(term[c, 2 * block : 2 * block + half], got_first[c, 1]).astype(BF16)
        second_copy(c, 0).start()
        for k in range(2, 4):
            first_copy(c, k).wait_recv()
        sum_out[c, 1] = add(term[c, block + half : 2 * block], got_first[c, 3]).astype(BF16)
        second_copy(c, 1).start()

    def send_home(c):
        second_copy(c, 0).wait_recv()
        second_copy(c, 1).wait_recv()
        low = add(term[c, 0:half], got_first[c, 0]) + got_second[c, 0].astype(F32)
        high = add(term[c, half:block], got_first[c, 2]) + got_second[c, 1].astype(F32)
        total = jnp.concatenate([low.astype(BF16), high.astype(BF16)], axis=0)
        stack = jnp.concatenate(
            [total[:, q * LANES : (q + 1) * LANES] for q in range(PARTS)], axis=0
        )
        out = dot_nn(spread_mat[...], stack).astype(BF16)
        ret[c] = out.reshape(n_expert, piece, LANES)
        for d in far_first:
            rz_copy(c, d).start()
        back[c, me_e] = ret[c, me_e]

    def finish(c):
        for d in far_first[::-1]:
            rz_copy(c, d).wait_recv()
        out = dot_nn(pick_back[...], back[c].reshape(n_expert * piece, LANES)).astype(BF16)
        for q in range(PARTS):
            tokens_ref[:, c * CHUNK + q * LANES : c * CHUNK + (q + 1) * LANES] = out[
                q * tok : (q + 1) * tok
            ]

    wide = score_part.shape[2]

    def sp_copy(j):
        return remote(
            score_part.at[j], score_got.at[j], sp_send.at[j], sp_recv.at[j], me_e, peers[j]
        )

    def sz_copy(d):
        dest = lax.rem(me_e + d, n_expert)
        return remote(
            score_tot, score_back.at[me_e], sz_send.at[d], sz_recv.at[d], dest, me_t
        )

    def send_scores():
        ones = jnp.ones((ROW_TILE, LANES), BF16)
        score_part[...] = jnp.zeros(score_part.shape, F32)
        for j in range(4):
            high, low = split_bf16(row_sum[j * block : (j + 1) * block, :])
            line = dot_nt(ones, high) + dot_nt(ones, low)
            score_part[j, :, 0:block] = line[0:8]
        for j in range(1, 4):
            sp_copy(j).start()

    def total_scores():
        for j in range(1, 4):
            sp_copy(j).wait_recv()
        score_tot[...] = (score_part[0] + score_got[1]) + (score_got[2] + score_got[3])
        for d in far_first:
            sz_copy(d).start()
        score_back[me_e] = score_tot[...]

    def finish_scores():
        for d in far_first:
            sz_copy(d).wait_recv()
        lane = iota((wide, tok), 0)
        pick = one_where(lane == me_e * cap + place)
        high, low = split_bf16(score_back[...].reshape(n_expert * 8, wide))
        mixed = dot_nn(high, pick) + dot_nn(low, pick)
        keep = iota((n_expert * 8, tok), 0) == routing * 8
        value = jnp.sum(jnp.where(keep, mixed, 0.0), axis=0, keepdims=True)
        score_out_ref[...] = (value / score).astype(BF16)

    finish_block(0)
    forward(n_chunk - 1)
    finish_block(1)
    first_block(1)
    first_copy(0, 0).start()
    finish_block(2)
    first_block(2)
    first_copy(0, 2).start()
    wait_diagonal(n_chunk - 1)
    finish_block(3)
    first_block(3)
    first_copy(0, 1).start()
    first_copy(0, 3).start()
    make_term(1)
    first_block(0)
    send_scores()
    second_stage(0)
    make_term(2)
    second_stage(1)
    send_home(0)
    down_term(0)
    make_term(3)
    second_stage(2)
    send_home(1)
    down_term(1)
    total_scores()
    make_term(4)
    second_stage(3)
    send_home(2)
    down_term(2)
    second_stage(4)
    send_home(3)
    finish(0)
    down_term(3)
    finish(1)
    down_term(4)
    send_home(4)
    finish(2)
    finish_scores()
    finish(3)
    finish(4)

    for c in range(n_chunk):
        for d in range(1, n_expert):
            z_copy(c, d).wait_send()
            rz_copy(c, d).wait_send()
        for k in range(4):
            ag_copy(c, k).wait_send()
            first_copy(c, k).wait_send()
        for k in range(2):
            second_copy(c, k).wait_send()
    for j in range(1, 4):
        sp_copy(j).wait_send()
    for d in range(1, n_expert):
        sz_copy(d).wait_send()


def hand_over(tokens_ref, score_ref, down_ref, tokens_out, score_out, down_out, out_sem):
    n_part = out_sem.shape[0] - 2
    height = down_ref.shape[1] // n_part
    pairs = [
        (down_ref.at[0, i * height : (i + 1) * height],
         down_out.at[0, i * height : (i + 1) * height])
        for i in range(n_part)
    ]
    pairs += [(tokens_ref, tokens_out), (score_ref, score_out)]
    outs = [pltpu.make_async_copy(a, b, out_sem.at[i]) for i, (a, b) in enumerate(pairs)]
    for out in outs:
        out.start()
    for out in outs:
        out.wait()


def fused_local(grad_out, router_score, routing, gate_pre, up_pre, gate_weight, up_weight, down_weight):
    n_expert = lax.axis_size("expert")
    tok, width = grad_out.shape
    cap = tok // n_expert + tok // (4 * n_expert)
    block = n_expert * cap
    piece = PARTS * cap
    n_rows = gate_pre.shape[1]
    hid = gate_pre.shape[2]
    n_chunk = width // CHUNK
    wide = -(-block // LANES) * LANES
    vmem = pl.BlockSpec(memory_space=pltpu.VMEM)
    hbm = pl.BlockSpec(memory_space=pl.ANY)
    dma = pltpu.SemaphoreType.DMA
    macs = 4 * n_rows * width * hid
    tokens, score, down = pl.pallas_call(
        functools.partial(kernel, n_expert, cap, n_chunk),
        out_shape=(
            pltpu.VMEM((tok, width), BF16),
            pltpu.VMEM((1, tok), BF16),
            pltpu.VMEM((1, hid, width), BF16),
        ),
        in_specs=[vmem, vmem, vmem, hbm, hbm, hbm, hbm, hbm],
        out_specs=(vmem, vmem, vmem),
        scratch_shapes=[
            pltpu.VMEM((width, hid), BF16),
            pltpu.VMEM((width, hid), BF16),
            pltpu.VMEM((hid, width), BF16),
            pltpu.VMEM((n_rows, hid), BF16),
            pltpu.VMEM((n_rows, hid), BF16),
            pltpu.VMEM((n_rows, hid), F32),
            pltpu.VMEM((n_rows, hid), F32),
            pltpu.VMEM((hid, n_rows), BF16),
            pltpu.VMEM((n_rows, hid), F32),
            pltpu.VMEM((n_rows, hid), BF16),
            pltpu.VMEM((n_rows, hid), BF16),
            pltpu.VMEM((n_expert * piece, PARTS * tok), BF16),
            pltpu.VMEM((PARTS * tok, n_expert * piece), BF16),
            pltpu.VMEM((PARTS * block, n_expert * piece), BF16),
            pltpu.VMEM((n_expert * piece, PARTS * block), BF16),
            pltpu.VMEM((n_chunk, n_expert, piece, LANES), BF16),
            pltpu.VMEM((n_chunk, n_expert, piece, LANES), BF16),
            pltpu.VMEM((n_chunk, n_rows, CHUNK), BF16),
            pltpu.VMEM((n_chunk, n_rows, CHUNK), BF16),
            pltpu.VMEM((n_chunk, 4, block // 2, CHUNK), BF16),
            pltpu.VMEM((n_chunk, 2, block // 2, CHUNK), BF16),
            pltpu.VMEM((n_chunk, 2, block // 2, CHUNK), BF16),
            pltpu.VMEM((n_chunk, n_expert, piece, LANES), BF16),
            pltpu.VMEM((n_chunk, n_expert, piece, LANES), BF16),
            pltpu.VMEM((n_rows, LANES), F32),
            pltpu.VMEM((4, 8, wide), F32),
            pltpu.VMEM((4, 8, wide), F32),
            pltpu.VMEM((8, wide), F32),
            pltpu.VMEM((n_expert, 8, wide), F32),
            dma((n_chunk, n_expert)),
            dma((n_chunk, n_expert)),
            dma((n_chunk, 4)),
            dma((n_chunk, 4)),
            dma((n_chunk, 4)),
            dma((n_chunk, 4)),
            dma((n_chunk, 2)),
            dma((n_chunk, 2)),
            dma((n_chunk, n_expert)),
            dma((n_chunk, n_expert)),
            dma((4,)),
            dma((4,)),
            dma((n_expert,)),
            dma((n_expert,)),
            dma((11,)),
        ],
        compiler_params=pltpu.CompilerParams(
            collective_id=0, has_side_effects=True, vmem_limit_bytes=54 * 1024 * 1024
        ),
        cost_estimate=pl.CostEstimate(
            flops=2 * macs,
            bytes_accessed=2 * (4 * width * hid + 2 * n_rows * hid),
            transcendentals=n_rows * hid,
        ),
        name="routed_backward",
    )(
        grad_out,
        router_score.reshape(1, tok),
        routing.reshape(1, tok),
        gate_pre,
        up_pre,
        gate_weight,
        up_weight,
        down_weight,
    )
    n_part = 4
    tokens, score, down = pl.pallas_call(
        hand_over,
        out_shape=(
            jax.ShapeDtypeStruct((tok, width), BF16),
            jax.ShapeDtypeStruct((1, tok), BF16),
            jax.ShapeDtypeStruct((1, hid, width), BF16),
        ),
        in_specs=[vmem, vmem, vmem],
        out_specs=(hbm, hbm, hbm),
        scratch_shapes=[dma((n_part + 2,))],
        name="hand_over",
    )(tokens, score, down)
    return tokens, score.reshape(tok), down


def fits(mesh, grad_out, gate_pre):
    n_expert, n_tensor = mesh.shape["expert"], mesh.shape["tensor"]
    tok = grad_out.shape[0] // (n_expert * n_tensor)
    cap = tok // n_expert + tok // (4 * n_expert)
    return (
        n_tensor == 4
        and n_expert <= ROW_TILE
        and cap % 4 == 0
        and (n_expert * cap) % 32 == 0
        and tok % LANES == 0
        and grad_out.shape[1] == 5 * CHUNK
        and gate_pre.shape[2] % (256 * n_tensor) == 0
    )


def expert_rows(rows_grad, rows_score, gate_rows, up_rows, down_local):
    through = lax.dot_general(
        rows_grad, down_local, (((1,), (1,)), ((), ())), preferred_element_type=jnp.float32
    )
    gate_val = gate_rows.astype(jnp.float32)
    up_val = up_rows.astype(jnp.float32)
    sig_gate = jax.nn.sigmoid(gate_val)
    hidden = gate_val * sig_gate * up_val
    part_score = jnp.sum(through * hidden, axis=1)
    scale_col = rows_score.astype(jnp.float32)[:, None]
    scaled = scale_col * through
    grad_gate = (scaled * up_val * sig_gate * (1.0 + gate_val * (1.0 - sig_gate))).astype(
        jnp.bfloat16
    )
    grad_up = (scaled * gate_val * sig_gate).astype(jnp.bfloat16)
    weighted = (scale_col * hidden).astype(jnp.bfloat16)
    down_term = lax.dot_general(
        weighted, rows_grad, (((0,), (0,)), ((), ())), preferred_element_type=jnp.float32
    )
    return (grad_gate, grad_up, part_score, down_term)


def local(grad_out, router_score, routing, gate_pre, up_pre, gate_weight, up_weight, down_weight):
    n_expert = lax.axis_size("expert")
    tok_count = grad_out.shape[0]
    width = grad_out.shape[1]
    capacity = tok_count // n_expert + tok_count // (4 * n_expert)
    slot_count = n_expert * capacity
    gate_local = gate_pre[0]
    up_local = up_pre[0]
    down_local = down_weight[0]
    gate_mat = gate_weight[0]
    up_mat = up_weight[0]
    expert_ids = routing[:, 0]
    onehot = (expert_ids[:, None] == jnp.arange(n_expert, dtype=jnp.int32)[None, :]).astype(
        jnp.int32
    )
    before = jnp.cumsum(onehot, axis=0) - onehot
    position = jnp.sum(before * onehot, axis=1)
    slot_index = expert_ids * capacity + position
    send_grad = jnp.zeros((slot_count, width), jnp.bfloat16).at[slot_index].set(grad_out)
    send_score = jnp.zeros((slot_count,), jnp.bfloat16).at[slot_index].set(router_score)
    recv_grad, recv_score = (
        lax.all_to_all(
            send_grad.reshape(n_expert, capacity, width),
            "expert",
            split_axis=0,
            concat_axis=0,
            tiled=True,
        ),
        lax.all_to_all(
            send_score.reshape(n_expert, capacity),
            "expert",
            split_axis=0,
            concat_axis=0,
            tiled=True,
        ),
    )
    recv_grad = recv_grad.reshape(slot_count, width)
    recv_score = recv_score.reshape(slot_count)
    all_grad, all_score = (
        lax.all_gather(recv_grad, "tensor", axis=0, tiled=True),
        lax.all_gather(recv_score, "tensor", axis=0, tiled=True),
    )
    grad_gate, grad_up, part_score, down_sum = expert_rows(
        all_grad, all_score, gate_local, up_local, down_local
    )
    term = lax.dot_general(
        grad_gate, gate_mat, (((1,), (1,)), ((), ())), preferred_element_type=jnp.float32
    )
    mine_grad = lax.psum_scatter(
        (
            term
            + lax.dot_general(
                grad_up, up_mat, (((1,), (1,)), ((), ())), preferred_element_type=jnp.float32
            )
        ).astype(jnp.bfloat16),
        "tensor",
        scatter_dimension=0,
        tiled=True,
    )
    mine_score = lax.psum_scatter(part_score, "tensor", scatter_dimension=0, tiled=True)
    back_grad, back_score = (
        lax.all_to_all(
            mine_grad.reshape(n_expert, capacity, width),
            "expert",
            split_axis=0,
            concat_axis=0,
            tiled=True,
        ),
        lax.all_to_all(
            mine_score.astype(jnp.bfloat16).reshape(n_expert, capacity),
            "expert",
            split_axis=0,
            concat_axis=0,
            tiled=True,
        ),
    )
    grad_tokens = back_grad.reshape(slot_count, width)[slot_index]
    grad_score = back_score.reshape(slot_count)[slot_index]
    grad_down_weight = down_sum.astype(jnp.bfloat16)[None]
    return (grad_tokens, grad_score, grad_down_weight)


def solution(mesh):
    def run(*arrays):
        body = fused_local if fits(mesh, arrays[0], arrays[3]) else local
        return jax.shard_map(
            body,
            mesh=mesh,
            in_specs=(
                P(("expert", "tensor"), None),
                P(("expert", "tensor")),
                P(("expert", "tensor"), None),
                P("expert", None, "tensor"),
                P("expert", None, "tensor"),
                P("expert", None, "tensor"),
                P("expert", None, "tensor"),
                P("expert", "tensor", None),
            ),
            out_specs=(
                P(("expert", "tensor"), None),
                P(("expert", "tensor")),
                P("expert", "tensor", None),
            ),
            check_vma=False,
        )(*arrays)

    return run
```

```python
import functools

import jax
import jax.numpy as jnp
from jax import lax
from jax.experimental import pallas as pl
from jax.experimental.pallas import tpu as pltpu
from jax.sharding import PartitionSpec as P

MESH = pl.DeviceIdType.MESH
LANES = 128
PARTS = 4
CHUNK = PARTS * LANES
ROW_TILE = 16
TILE = 256
F32 = jnp.float32
BF16 = jnp.bfloat16


def dot_nn(a, b):
    return lax.dot_general(a, b, (((1,), (0,)), ((), ())), preferred_element_type=F32)


def dot_nt(a, b):
    return lax.dot_general(a, b, (((1,), (1,)), ((), ())), preferred_element_type=F32)


def dot_tn(a, b):
    return lax.dot_general(a, b, (((0,), (0,)), ((), ())), preferred_element_type=F32)


def split_bf16(value):
    high = value.astype(BF16)
    return high, (value - high.astype(F32)).astype(BF16)


def iota(shape, dim):
    return lax.broadcasted_iota(jnp.int32, shape, dim)


def one_where(mask):
    return jnp.where(mask, 1.0, 0.0).astype(BF16)


def kernel(
    n_expert, cap, n_chunk,
    grad_ref, score_ref, routing_ref, gate_pre_ref, up_pre_ref, gate_w_ref, up_w_ref, down_w_ref,
    tokens_ref, score_out_ref, down_out_ref,
    gate_w, up_w, down_w, gate_v, up_v, coef_gate, coef_up, hidden_t, through, grad_gate, grad_up,
    pick_send, pick_back, gather_mat, spread_mat,
    send, recv, rows, term, got_first, sum_out, got_second, ret, back,
    row_sum, score_part, score_got, score_tot, score_back,
    z_send, z_recv, ag_send, ag_recv, first_send, first_recv, second_send, second_recv,
    rz_send, rz_recv, sp_send, sp_recv, sz_send, sz_recv, load_sem,
):
    tok = grad_ref.shape[0]
    block = n_expert * cap
    half = block // 2
    piece = PARTS * cap
    n_rows = PARTS * block
    hid = gate_v.shape[1]
    me_e = lax.axis_index("expert")
    me_t = lax.axis_index("tensor")
    near = me_t + 1 - 2 * lax.rem(me_t, 2)
    over = lax.rem(me_t + 2, 4)
    td = 3 - me_t
    odd = lax.rem(me_e, 2)
    tx = near + odd * (over - near)
    ty = over + odd * (near - over)
    peers = (me_t, tx, ty, td)

    barrier = pltpu.get_barrier_semaphore()
    for d in range(1, n_expert):
        pl.semaphore_signal(
            barrier, inc=1, device_id=(lax.rem(me_e + d, n_expert), me_t), device_id_type=MESH
        )
    for j in range(1, 4):
        pl.semaphore_signal(barrier, inc=1, device_id=(me_e, peers[j]), device_id_type=MESH)

    loads = []
    for j in range(4):
        start = pl.multiple_of(peers[j] * block, block)
        for k, (src, dst) in enumerate(((gate_pre_ref, gate_v), (up_pre_ref, up_v))):
            loads.append(
                pltpu.make_async_copy(
                    src.at[0, pl.ds(start, block)],
                    dst.at[pl.ds(j * block, block)],
                    load_sem.at[2 * j + k],
                )
            )
    load_down = pltpu.make_async_copy(down_w_ref.at[0], down_w, load_sem.at[8])
    load_gate = pltpu.make_async_copy(gate_w_ref.at[0], gate_w, load_sem.at[9])
    load_up = pltpu.make_async_copy(up_w_ref.at[0], up_w, load_sem.at[10])
    for copy in loads + [load_down, load_gate, load_up]:
        copy.start()

    def remote(src, dst, s_sem, r_sem, e, t):
        return pltpu.make_async_remote_copy(
            src_ref=src, dst_ref=dst, send_sem=s_sem, recv_sem=r_sem,
            device_id=(e, t), device_id_type=MESH,
        )

    routing = routing_ref[...]
    named = iota((ROW_TILE, tok), 0) == routing
    earlier = one_where(iota((tok, tok), 0) < iota((tok, tok), 1))
    before = dot_nn(one_where(named), earlier)
    place = jnp.sum(jnp.where(named, before, 0.0), axis=0, keepdims=True).astype(jnp.int32)
    key = routing * piece + place
    score = score_ref[...].astype(F32)
    spot = iota((n_expert * piece, tok), 0)
    for q in range(PARTS):
        pick_send[:, q * tok : (q + 1) * tok] = jnp.where(
            spot == key + q * cap, score, 0.0
        ).astype(BF16)

    def z_copy(c, d):
        dest = lax.rem(me_e + d, n_expert)
        return remote(
            send.at[c, dest], recv.at[c, me_e], z_send.at[c, d], z_recv.at[c, d], dest, me_t
        )

    far_first = sorted(range(1, n_expert), key=lambda d: -min(d, n_expert - d))

    def dispatch(c):
        stack = jnp.concatenate(
            [
                grad_ref[:, c * CHUNK + q * LANES : c * CHUNK + (q + 1) * LANES]
                for q in range(PARTS)
            ],
            axis=0,
        )
        out = dot_nn(pick_send[...], stack).astype(BF16)
        send[c] = out.reshape(n_expert, piece, LANES)
        if c == 0:
            pl.semaphore_wait(barrier, n_expert - 1 + 3)
        for d in far_first:
            z_copy(c, d).start()
        recv[c, me_e] = send[c, me_e]

    dispatch(0)
    dispatch(1)

    key_f = key.astype(F32)
    key_col = jnp.sum(
        jnp.where(iota((tok, tok), 0) == iota((tok, tok), 1), key_f, 0.0), axis=1, keepdims=True
    ).astype(jnp.int32)
    lane_spot = iota((tok, n_expert * piece), 1)
    for q in range(PARTS):
        pick_back[q * tok : (q + 1) * tok, :] = one_where(lane_spot == key_col + q * cap)
    for q in range(PARTS):
        r = iota((block, n_expert * piece), 0)
        s = sum((r >= k * cap).astype(jnp.int32) for k in range(1, n_expert))
        gather_mat[q * block : (q + 1) * block, :] = one_where(
            iota((block, n_expert * piece), 1) == r + s * (piece - cap) + q * cap
        )
    spread_mat[...] = gather_mat[...].T

    def ag_copy(c, k):
        if k == 0:
            src, dst, t = rows.at[c, 0:block], rows.at[c, block : 2 * block], tx
        elif k == 1:
            src, dst, t = rows.at[c, 0:block], rows.at[c, 2 * block : 3 * block], ty
        elif k == 2:
            src, dst, t = (
                rows.at[c, block : block + half], rows.at[c, 3 * block : 3 * block + half], ty
            )
        else:
            src, dst, t = (
                rows.at[c, 2 * block + half : 3 * block],
                rows.at[c, 3 * block + half : 4 * block],
                tx,
            )
        return remote(src, dst, ag_send.at[c, k], ag_recv.at[c, k], me_e, t)

    def arrive(c):
        for d in far_first[::-1]:
            z_copy(c, d).wait_recv()
        pieces = recv[c].reshape(n_expert * piece, LANES)
        out = dot_nn(gather_mat[...], pieces).astype(BF16)
        for q in range(PARTS):
            rows[c, 0:block, q * LANES : (q + 1) * LANES] = out[q * block : (q + 1) * block]
        ag_copy(c, 0).start()
        ag_copy(c, 1).start()

    def forward(c):
        ag_copy(c, 0).wait_recv()
        ag_copy(c, 2).start()
        ag_copy(c, 1).wait_recv()
        ag_copy(c, 3).start()

    def wait_diagonal(c):
        ag_copy(c, 2).wait_recv()
        ag_copy(c, 3).wait_recv()

    def through_part(c):
        wait_diagonal(c)

        def body(i, carry):
            at = pl.ds(pl.multiple_of(i * TILE, TILE), TILE)
            part = dot_nt(rows[c], down_w[at, c * CHUNK : (c + 1) * CHUNK])
            if c == 0:
                through[:, at] = part
            else:
                through[:, at] = through[:, at] + part
            return carry

        lax.fori_loop(0, hid // TILE, body, 0)

    def down_term(c):
        def body(i, carry):
            at = pl.ds(pl.multiple_of(i * TILE, TILE), TILE)
            to = pl.ds(pl.multiple_of(c * CHUNK + i * TILE, TILE), TILE)
            down_out_ref[0, :, to] = dot_nn(hidden_t[...], rows[c, :, at]).astype(BF16)
            return carry

        lax.fori_loop(0, CHUNK // TILE, body, 0)

    def coefficients():
        for copy in loads:
            copy.wait()

        def body(i, carry):
            at = pl.ds(pl.multiple_of(i * ROW_TILE, ROW_TILE), ROW_TILE)
            gate = gate_v[at, :].astype(F32)
            up = up_v[at, :].astype(F32)
            sig = lax.logistic(gate)
            silu = gate * sig
            coef_up[at, :] = silu
            coef_gate[at, :] = up * sig * (1.0 + gate * (1.0 - sig))
            grad_up[at, :] = (silu * up).astype(BF16)
            return carry

        lax.fori_loop(0, n_rows // ROW_TILE, body, 0)

        def turn(i, carry):
            at = pl.ds(pl.multiple_of(i * LANES, LANES), LANES)
            hidden_t[:, at] = grad_up[at, :].T
            return carry

        lax.fori_loop(0, n_rows // LANES, turn, 0)

    arrive(0)
    dispatch(2)
    arrive(1)
    dispatch(3)
    coefficients()
    forward(0)
    arrive(2)
    dispatch(4)
    load_down.wait()
    forward(1)
    through_part(0)
    arrive(3)
    forward(2)
    through_part(1)
    arrive(4)
    forward(3)
    through_part(2)
    load_gate.wait()
    load_up.wait()
    through_part(3)

    def grads(i, carry):
        at = pl.ds(pl.multiple_of(i * ROW_TILE, ROW_TILE), ROW_TILE)
        value = through[at, :]
        silu = coef_up[at, :]
        grad_gate[at, :] = (value * coef_gate[at, :]).astype(BF16)
        grad_up[at, :] = (value * silu).astype(BF16)
        prod = value * silu * up_v[at, :].astype(F32)
        total = prod[:, 0:LANES]
        for k in range(1, hid // LANES):
            total = total + prod[:, k * LANES : (k + 1) * LANES]
        row_sum[at, :] = total
        return carry

    def finish_block(j):
        last = n_chunk - 1
        span = slice(j * block, (j + 1) * block)

        def body(i, carry):
            at = pl.ds(pl.multiple_of(i * TILE, TILE), TILE)
            part = dot_nt(rows[last, span, :], down_w[at, last * CHUNK : (last + 1) * CHUNK])
            through[span, at] = through[span, at] + part
            return carry

        lax.fori_loop(0, hid // TILE, body, 0)
        per = block // ROW_TILE
        lax.fori_loop(j * per, (j + 1) * per, grads, 0)

    def first_copy(c, k):
        begin = ((block, tx), (3 * block, tx), (2 * block + half, ty), (3 * block + half, ty))[k]
        return remote(
            term.at[c, begin[0] : begin[0] + half], got_first.at[c, k],
            first_send.at[c, k], first_recv.at[c, k], me_e, begin[1],
        )

    def second_copy(c, k):
        return remote(
            sum_out.at[c, k], got_second.at[c, k],
            second_send.at[c, k], second_recv.at[c, k], me_e, (ty, tx)[k],
        )

    def rz_copy(c, d):
        dest = lax.rem(me_e + d, n_expert)
        return remote(
            ret.at[c, dest], back.at[c, me_e], rz_send.at[c, d], rz_recv.at[c, d], dest, me_t
        )

    def make_term(c):
        for n in range(CHUNK // TILE):
            at = slice(c * CHUNK + n * TILE, c * CHUNK + (n + 1) * TILE)

            def body(j, carry):
                span = pl.ds(pl.multiple_of(j * 2 * block, 2 * block), 2 * block)
                value = dot_nt(grad_gate[span, :], gate_w[at, :])
                value = value + dot_nt(grad_up[span, :], up_w[at, :])
                term[c, span, n * TILE : (n + 1) * TILE] = value.astype(BF16)
                return carry

            lax.fori_loop(0, 2, body, 0)
        for k in (0, 2, 1, 3):
            first_copy(c, k).start()

    def first_block(j):
        span = slice(j * block, (j + 1) * block)

        def body(i, carry):
            at = pl.ds(pl.multiple_of(i * TILE, TILE), TILE)
            value = dot_nt(grad_gate[span, :], gate_w[at, :])
            value = value + dot_nt(grad_up[span, :], up_w[at, :])
            term[0, span, at] = value.astype(BF16)
            return carry

        lax.fori_loop(0, CHUNK // TILE, body, 0)

    def add(a, b):
        return a.astype(F32) + b.astype(F32)

    def second_stage(c):
        for k in range(2):
            first_copy(c, k).wait_recv()
        sum_out[c, 0] = add(term[c, 2 * block : 2 * block + half], got_first[c, 1]).astype(BF16)
        second_copy(c, 0).start()
        for k in range(2, 4):
            first_copy(c, k).wait_recv()
        sum_out[c, 1] = add(term[c, block + half : 2 * block], got_first[c, 3]).astype(BF16)
        second_copy(c, 1).start()

    def send_home(c):
        second_copy(c, 0).wait_recv()
        second_copy(c, 1).wait_recv()
        low = add(term[c, 0:half], got_first[c, 0]) + got_second[c, 0].astype(F32)
        high = add(term[c, half:block], got_first[c, 2]) + got_second[c, 1].astype(F32)
        total = jnp.concatenate([low.astype(BF16), high.astype(BF16)], axis=0)
        stack = jnp.concatenate(
            [total[:, q * LANES : (q + 1) * LANES] for q in range(PARTS)], axis=0
        )
        out = dot_nn(spread_mat[...], stack).astype(BF16)
        ret[c] = out.reshape(n_expert, piece, LANES)
        for d in far_first:
            rz_copy(c, d).start()
        back[c, me_e] = ret[c, me_e]

    def finish(c):
        for d in far_first[::-1]:
            rz_copy(c, d).wait_recv()
        out = dot_nn(pick_back[...], back[c].reshape(n_expert * piece, LANES)).astype(BF16)
        for q in range(PARTS):
            tokens_ref[:, c * CHUNK + q * LANES : c * CHUNK + (q + 1) * LANES] = out[
                q * tok : (q + 1) * tok
            ]

    wide = score_part.shape[2]

    def sp_copy(j):
        return remote(
            score_part.at[j], score_got.at[j], sp_send.at[j], sp_recv.at[j], me_e, peers[j]
        )

    def sz_copy(d):
        dest = lax.rem(me_e + d, n_expert)
        return remote(
            score_tot, score_back.at[me_e], sz_send.at[d], sz_recv.at[d], dest, me_t
        )

    def send_scores():
        ones = jnp.ones((ROW_TILE, LANES), BF16)
        score_part[...] = jnp.zeros(score_part.shape, F32)
        for j in range(4):
            high, low = split_bf16(row_sum[j * block : (j + 1) * block, :])
            line = dot_nt(ones, high) + dot_nt(ones, low)
            score_part[j, :, 0:block] = line[0:8]
        for j in range(1, 4):
            sp_copy(j).start()

    def total_scores():
        for j in range(1, 4):
            sp_copy(j).wait_recv()
        score_tot[...] = (score_part[0] + score_got[1]) + (score_got[2] + score_got[3])
        for d in far_first:
            sz_copy(d).start()
        score_back[me_e] = score_tot[...]

    def finish_scores():
        for d in far_first:
            sz_copy(d).wait_recv()
        lane = iota((wide, tok), 0)
        pick = one_where(lane == me_e * cap + place)
        high, low = split_bf16(score_back[...].reshape(n_expert * 8, wide))
        mixed = dot_nn(high, pick) + dot_nn(low, pick)
        keep = iota((n_expert * 8, tok), 0) == routing * 8
        value = jnp.sum(jnp.where(keep, mixed, 0.0), axis=0, keepdims=True)
        score_out_ref[...] = (value / score).astype(BF16)

    finish_block(0)
    forward(n_chunk - 1)
    finish_block(1)
    first_block(1)
    first_copy(0, 0).start()
    finish_block(2)
    first_block(2)
    first_copy(0, 2).start()
    wait_diagonal(n_chunk - 1)
    finish_block(3)
    first_block(3)
    first_copy(0, 1).start()
    first_copy(0, 3).start()
    make_term(1)
    first_block(0)
    send_scores()
    second_stage(0)
    make_term(2)
    second_stage(1)
    send_home(0)
    down_term(0)
    make_term(3)
    second_stage(2)
    send_home(1)
    down_term(1)
    total_scores()
    make_term(4)
    second_stage(3)
    send_home(2)
    down_term(2)
    second_stage(4)
    send_home(3)
    finish(0)
    down_term(3)
    finish(1)
    down_term(4)
    send_home(4)
    finish(2)
    finish_scores()
    finish(3)
    finish(4)

    for c in range(n_chunk):
        for d in range(1, n_expert):
            z_copy(c, d).wait_send()
            rz_copy(c, d).wait_send()
        for k in range(4):
            ag_copy(c, k).wait_send()
            first_copy(c, k).wait_send()
        for k in range(2):
            second_copy(c, k).wait_send()
    for j in range(1, 4):
        sp_copy(j).wait_send()
    for d in range(1, n_expert):
        sz_copy(d).wait_send()


def hand_over(tokens_ref, score_ref, down_ref, tokens_out, score_out, down_out, out_sem):
    n_part = out_sem.shape[0] - 2
    height = down_ref.shape[1] // n_part
    pairs = [
        (down_ref.at[0, i * height : (i + 1) * height],
         down_out.at[0, i * height : (i + 1) * height])
        for i in range(n_part)
    ]
    pairs += [(tokens_ref, tokens_out), (score_ref, score_out)]
    outs = [pltpu.make_async_copy(a, b, out_sem.at[i]) for i, (a, b) in enumerate(pairs)]
    for out in outs:
        out.start()
    for out in outs:
        out.wait()


def fused_local(grad_out, router_score, routing, gate_pre, up_pre, gate_weight, up_weight, down_weight):
    n_expert = lax.axis_size("expert")
    tok, width = grad_out.shape
    cap = tok // n_expert + tok // (4 * n_expert)
    block = n_expert * cap
    piece = PARTS * cap
    n_rows = gate_pre.shape[1]
    hid = gate_pre.shape[2]
    n_chunk = width // CHUNK
    wide = -(-block // LANES) * LANES
    vmem = pl.BlockSpec(memory_space=pltpu.VMEM)
    hbm = pl.BlockSpec(memory_space=pl.ANY)
    dma = pltpu.SemaphoreType.DMA
    macs = 4 * n_rows * width * hid
    tokens, score, down = pl.pallas_call(
        functools.partial(kernel, n_expert, cap, n_chunk),
        out_shape=(
            pltpu.VMEM((tok, width), BF16),
            pltpu.VMEM((1, tok), BF16),
            pltpu.VMEM((1, hid, width), BF16),
        ),
        in_specs=[vmem, vmem, vmem, hbm, hbm, hbm, hbm, hbm],
        out_specs=(vmem, vmem, vmem),
        scratch_shapes=[
            pltpu.VMEM((width, hid), BF16),
            pltpu.VMEM((width, hid), BF16),
            pltpu.VMEM((hid, width), BF16),
            pltpu.VMEM((n_rows, hid), BF16),
            pltpu.VMEM((n_rows, hid), BF16),
            pltpu.VMEM((n_rows, hid), F32),
            pltpu.VMEM((n_rows, hid), F32),
            pltpu.VMEM((hid, n_rows), BF16),
            pltpu.VMEM((n_rows, hid), F32),
            pltpu.VMEM((n_rows, hid), BF16),
            pltpu.VMEM((n_rows, hid), BF16),
            pltpu.VMEM((n_expert * piece, PARTS * tok), BF16),
            pltpu.VMEM((PARTS * tok, n_expert * piece), BF16),
            pltpu.VMEM((PARTS * block, n_expert * piece), BF16),
            pltpu.VMEM((n_expert * piece, PARTS * block), BF16),
            pltpu.VMEM((n_chunk, n_expert, piece, LANES), BF16),
            pltpu.VMEM((n_chunk, n_expert, piece, LANES), BF16),
            pltpu.VMEM((n_chunk, n_rows, CHUNK), BF16),
            pltpu.VMEM((n_chunk, n_rows, CHUNK), BF16),
            pltpu.VMEM((n_chunk, 4, block // 2, CHUNK), BF16),
            pltpu.VMEM((n_chunk, 2, block // 2, CHUNK), BF16),
            pltpu.VMEM((n_chunk, 2, block // 2, CHUNK), BF16),
            pltpu.VMEM((n_chunk, n_expert, piece, LANES), BF16),
            pltpu.VMEM((n_chunk, n_expert, piece, LANES), BF16),
            pltpu.VMEM((n_rows, LANES), F32),
            pltpu.VMEM((4, 8, wide), F32),
            pltpu.VMEM((4, 8, wide), F32),
            pltpu.VMEM((8, wide), F32),
            pltpu.VMEM((n_expert, 8, wide), F32),
            dma((n_chunk, n_expert)),
            dma((n_chunk, n_expert)),
            dma((n_chunk, 4)),
            dma((n_chunk, 4)),
            dma((n_chunk, 4)),
            dma((n_chunk, 4)),
            dma((n_chunk, 2)),
            dma((n_chunk, 2)),
            dma((n_chunk, n_expert)),
            dma((n_chunk, n_expert)),
            dma((4,)),
            dma((4,)),
            dma((n_expert,)),
            dma((n_expert,)),
            dma((11,)),
        ],
        compiler_params=pltpu.CompilerParams(
            collective_id=0, has_side_effects=True, vmem_limit_bytes=54 * 1024 * 1024
        ),
        cost_estimate=pl.CostEstimate(
            flops=2 * macs,
            bytes_accessed=2 * (4 * width * hid + 2 * n_rows * hid),
            transcendentals=n_rows * hid,
        ),
        name="routed_backward",
    )(
        grad_out,
        router_score.reshape(1, tok),
        routing.reshape(1, tok),
        gate_pre,
        up_pre,
        gate_weight,
        up_weight,
        down_weight,
    )
    n_part = 4
    tokens, score, down = pl.pallas_call(
        hand_over,
        out_shape=(
            jax.ShapeDtypeStruct((tok, width), BF16),
            jax.ShapeDtypeStruct((1, tok), BF16),
            jax.ShapeDtypeStruct((1, hid, width), BF16),
        ),
        in_specs=[vmem, vmem, vmem],
        out_specs=(hbm, hbm, hbm),
        scratch_shapes=[dma((n_part + 2,))],
        compiler_params=pltpu.CompilerParams(vmem_limit_bytes=1024 * 1024),
        name="hand_over",
    )(tokens, score, down)
    return tokens, score.reshape(tok), down


def fits(mesh, grad_out, gate_pre):
    n_expert, n_tensor = mesh.shape["expert"], mesh.shape["tensor"]
    tok = grad_out.shape[0] // (n_expert * n_tensor)
    cap = tok // n_expert + tok // (4 * n_expert)
    return (
        n_tensor == 4
        and n_expert <= ROW_TILE
        and cap % 4 == 0
        and (n_expert * cap) % 32 == 0
        and tok % LANES == 0
        and grad_out.shape[1] == 5 * CHUNK
        and gate_pre.shape[2] % (256 * n_tensor) == 0
    )


def expert_rows(rows_grad, rows_score, gate_rows, up_rows, down_local):
    through = lax.dot_general(
        rows_grad, down_local, (((1,), (1,)), ((), ())), preferred_element_type=jnp.float32
    )
    gate_val = gate_rows.astype(jnp.float32)
    up_val = up_rows.astype(jnp.float32)
    sig_gate = jax.nn.sigmoid(gate_val)
    hidden = gate_val * sig_gate * up_val
    part_score = jnp.sum(through * hidden, axis=1)
    scale_col = rows_score.astype(jnp.float32)[:, None]
    scaled = scale_col * through
    grad_gate = (scaled * up_val * sig_gate * (1.0 + gate_val * (1.0 - sig_gate))).astype(
        jnp.bfloat16
    )
    grad_up = (scaled * gate_val * sig_gate).astype(jnp.bfloat16)
    weighted = (scale_col * hidden).astype(jnp.bfloat16)
    down_term = lax.dot_general(
        weighted, rows_grad, (((0,), (0,)), ((), ())), preferred_element_type=jnp.float32
    )
    return (grad_gate, grad_up, part_score, down_term)


def local(grad_out, router_score, routing, gate_pre, up_pre, gate_weight, up_weight, down_weight):
    n_expert = lax.axis_size("expert")
    tok_count = grad_out.shape[0]
    width = grad_out.shape[1]
    capacity = tok_count // n_expert + tok_count // (4 * n_expert)
    slot_count = n_expert * capacity
    gate_local = gate_pre[0]
    up_local = up_pre[0]
    down_local = down_weight[0]
    gate_mat = gate_weight[0]
    up_mat = up_weight[0]
    expert_ids = routing[:, 0]
    onehot = (expert_ids[:, None] == jnp.arange(n_expert, dtype=jnp.int32)[None, :]).astype(
        jnp.int32
    )
    before = jnp.cumsum(onehot, axis=0) - onehot
    position = jnp.sum(before * onehot, axis=1)
    slot_index = expert_ids * capacity + position
    send_grad = jnp.zeros((slot_count, width), jnp.bfloat16).at[slot_index].set(grad_out)
    send_score = jnp.zeros((slot_count,), jnp.bfloat16).at[slot_index].set(router_score)
    recv_grad, recv_score = (
        lax.all_to_all(
            send_grad.reshape(n_expert, capacity, width),
            "expert",
            split_axis=0,
            concat_axis=0,
            tiled=True,
        ),
        lax.all_to_all(
            send_score.reshape(n_expert, capacity),
            "expert",
            split_axis=0,
            concat_axis=0,
            tiled=True,
        ),
    )
    recv_grad = recv_grad.reshape(slot_count, width)
    recv_score = recv_score.reshape(slot_count)
    all_grad, all_score = (
        lax.all_gather(recv_grad, "tensor", axis=0, tiled=True),
        lax.all_gather(recv_score, "tensor", axis=0, tiled=True),
    )
    grad_gate, grad_up, part_score, down_sum = expert_rows(
        all_grad, all_score, gate_local, up_local, down_local
    )
    term = lax.dot_general(
        grad_gate, gate_mat, (((1,), (1,)), ((), ())), preferred_element_type=jnp.float32
    )
    mine_grad = lax.psum_scatter(
        (
            term
            + lax.dot_general(
                grad_up, up_mat, (((1,), (1,)), ((), ())), preferred_element_type=jnp.float32
            )
        ).astype(jnp.bfloat16),
        "tensor",
        scatter_dimension=0,
        tiled=True,
    )
    mine_score = lax.psum_scatter(part_score, "tensor", scatter_dimension=0, tiled=True)
    back_grad, back_score = (
        lax.all_to_all(
            mine_grad.reshape(n_expert, capacity, width),
            "expert",
            split_axis=0,
            concat_axis=0,
            tiled=True,
        ),
        lax.all_to_all(
            mine_score.astype(jnp.bfloat16).reshape(n_expert, capacity),
            "expert",
            split_axis=0,
            concat_axis=0,
            tiled=True,
        ),
    )
    grad_tokens = back_grad.reshape(slot_count, width)[slot_index]
    grad_score = back_score.reshape(slot_count)[slot_index]
    grad_down_weight = down_sum.astype(jnp.bfloat16)[None]
    return (grad_tokens, grad_score, grad_down_weight)


def solution(mesh):
    def run(*arrays):
        body = fused_local if fits(mesh, arrays[0], arrays[3]) else local
        return jax.shard_map(
            body,
            mesh=mesh,
            in_specs=(
                P(("expert", "tensor"), None),
                P(("expert", "tensor")),
                P(("expert", "tensor"), None),
                P("expert", None, "tensor"),
                P("expert", None, "tensor"),
                P("expert", None, "tensor"),
                P("expert", None, "tensor"),
                P("expert", "tensor", None),
            ),
            out_specs=(
                P(("expert", "tensor"), None),
                P(("expert", "tensor")),
                P("expert", "tensor", None),
            ),
            check_vma=False,
        )(*arrays)

    return run
```

```python
import functools

import jax
import jax.numpy as jnp
from jax import lax
from jax.experimental import pallas as pl
from jax.experimental.pallas import tpu as pltpu
from jax.sharding import PartitionSpec as P

MESH = pl.DeviceIdType.MESH
LANES = 128
PARTS = 4
CHUNK = PARTS * LANES
ROW_TILE = 16
TILE = 256
F32 = jnp.float32
BF16 = jnp.bfloat16


def dot_nn(a, b):
    return lax.dot_general(a, b, (((1,), (0,)), ((), ())), preferred_element_type=F32)


def dot_nt(a, b):
    return lax.dot_general(a, b, (((1,), (1,)), ((), ())), preferred_element_type=F32)


def dot_tn(a, b):
    return lax.dot_general(a, b, (((0,), (0,)), ((), ())), preferred_element_type=F32)


def split_bf16(value):
    high = value.astype(BF16)
    return high, (value - high.astype(F32)).astype(BF16)


def iota(shape, dim):
    return lax.broadcasted_iota(jnp.int32, shape, dim)


def one_where(mask):
    return jnp.where(mask, 1.0, 0.0).astype(BF16)


def kernel(
    n_expert, cap, n_chunk,
    grad_ref, score_ref, routing_ref, gate_pre_ref, up_pre_ref, gate_w_ref, up_w_ref, down_w_ref,
    tokens_ref, score_out_ref, down_out_ref,
    gate_w, up_w, down_w, gate_v, up_v, coef_gate, coef_up, hidden_t, through, grad_gate, grad_up,
    pick_send, pick_back, gather_mat, spread_mat,
    send, local_p, remote_p, rows, term, got_first, sum_out, got_second, ret, back,
    row_sum, score_part, score_got, score_tot, score_back,
    z_send, z_recv, lg_send, lg_recv, ag_send, ag_recv, first_send, first_recv, second_send, second_recv,
    rz_send, rz_recv, sp_send, sp_recv, sz_send, sz_recv, load_sem,
):
    tok = grad_ref.shape[0]
    block = n_expert * cap
    half = block // 2
    piece = PARTS * cap
    n_rows = PARTS * block
    hid = gate_v.shape[1]
    me_e = lax.axis_index("expert")
    me_t = lax.axis_index("tensor")
    near = me_t + 1 - 2 * lax.rem(me_t, 2)
    over = lax.rem(me_t + 2, 4)
    td = 3 - me_t
    odd = lax.rem(me_e, 2)
    tx = near + odd * (over - near)
    ty = over + odd * (near - over)
    peers = (me_t, tx, ty, td)

    barrier = pltpu.get_barrier_semaphore()
    for d in range(1, n_expert):
        pl.semaphore_signal(
            barrier, inc=1, device_id=(lax.rem(me_e + d, n_expert), me_t), device_id_type=MESH
        )
    for j in range(1, 4):
        pl.semaphore_signal(barrier, inc=1, device_id=(me_e, peers[j]), device_id_type=MESH)

    loads = []
    for j in range(4):
        start = pl.multiple_of(peers[j] * block, block)
        for k, (src, dst) in enumerate(((gate_pre_ref, gate_v), (up_pre_ref, up_v))):
            loads.append(
                pltpu.make_async_copy(
                    src.at[0, pl.ds(start, block)],
                    dst.at[pl.ds(j * block, block)],
                    load_sem.at[2 * j + k],
                )
            )
    load_down = pltpu.make_async_copy(down_w_ref.at[0], down_w, load_sem.at[8])
    load_gate = pltpu.make_async_copy(gate_w_ref.at[0], gate_w, load_sem.at[9])
    load_up = pltpu.make_async_copy(up_w_ref.at[0], up_w, load_sem.at[10])
    for copy in loads + [load_down, load_gate, load_up]:
        copy.start()

    def remote(src, dst, s_sem, r_sem, e, t):
        return pltpu.make_async_remote_copy(
            src_ref=src, dst_ref=dst, send_sem=s_sem, recv_sem=r_sem,
            device_id=(e, t), device_id_type=MESH,
        )

    routing = routing_ref[...]
    named = iota((ROW_TILE, tok), 0) == routing
    earlier = one_where(iota((tok, tok), 0) < iota((tok, tok), 1))
    before = dot_nn(one_where(named), earlier)
    place = jnp.sum(jnp.where(named, before, 0.0), axis=0, keepdims=True).astype(jnp.int32)
    key = routing * piece + place
    score = score_ref[...].astype(F32)
    spot = iota((n_expert * piece, tok), 0)
    for q in range(PARTS):
        pick_send[:, q * tok : (q + 1) * tok] = jnp.where(
            spot == key + q * cap, score, 0.0
        ).astype(BF16)

    plane = me_e // 2
    core = lax.rem(me_e, 2)
    n_plane = n_expert // 2

    def z_copy(c, dz, dc):
        dest = lax.rem(plane + dz, n_plane) * 2 + lax.rem(core + dc, 2)
        seen = (n_plane - dz) % n_plane
        if dz == 0:
            landing = local_p.at[0, core, c]
        else:
            landing = remote_p.at[0, c, (seen - 1) * 2 + core]
        return remote(
            send.at[c, dest], landing, z_send.at[c, 2 * dz + dc], z_recv.at[c, 2 * seen + dc],
            dest, me_t,
        )

    far_first = sorted(range(1, n_expert), key=lambda d: -min(d, n_expert - d))
    z_order = sorted(range(1, n_plane), key=lambda d: -min(d, n_plane - d))

    def dispatch(c):
        stack = jnp.concatenate(
            [
                grad_ref[:, c * CHUNK + q * LANES : c * CHUNK + (q + 1) * LANES]
                for q in range(PARTS)
            ],
            axis=0,
        )
        out = dot_nn(pick_send[...], stack).astype(BF16)
        send[c] = out.reshape(n_expert, piece, LANES)
        if c == 0:
            pl.semaphore_wait(barrier, n_expert - 1 + 3)
        z_copy(c, 0, 1).start()
        local_p[0, core, c] = send[c, me_e]

    def send_far(c):
        for dz in z_order:
            z_copy(c, dz, 0).start()
            z_copy(c, dz, 1).start()

    def local_copy(k):
        src, dst, t = (
            (local_p.at[0], local_p.at[1], tx),
            (local_p.at[0], local_p.at[2], ty),
            (local_p.at[1, 0], local_p.at[3, 0], ty),
            (local_p.at[2, 1], local_p.at[3, 1], tx),
        )[k]
        return remote(src, dst, lg_send.at[k], lg_recv.at[k], me_e, t)

    dispatch(0)
    send_far(0)
    dispatch(1)
    send_far(1)
    for c in range(2, n_chunk):
        dispatch(c)
    for c in range(n_chunk):
        z_copy(c, 0, 1).wait_recv()
    local_copy(0).start()
    local_copy(1).start()

    key_f = key.astype(F32)
    key_col = jnp.sum(
        jnp.where(iota((tok, tok), 0) == iota((tok, tok), 1), key_f, 0.0), axis=1, keepdims=True
    ).astype(jnp.int32)
    lane_spot = iota((tok, n_expert * piece), 1)
    for q in range(PARTS):
        pick_back[q * tok : (q + 1) * tok, :] = one_where(lane_spot == key_col + q * cap)
    for q in range(PARTS):
        r = iota((block, n_expert * piece), 0)
        s = sum((r >= k * cap).astype(jnp.int32) for k in range(1, n_expert))
        lane = iota((block, n_expert * piece), 1)
        at = slice(q * block, (q + 1) * block)
        spot_abs = r + s * (piece - cap) + q * cap
        spread_t = one_where(lane == spot_abs)
        shift = spot_abs - 2 * piece * plane
        shift = jnp.where(shift < 0, shift + n_expert * piece, shift)
        spread_mat[:, at] = spread_t.T
        gather_mat[at, :] = one_where(lane == shift)

    def ag_copy(c, k):
        n_far = n_expert - 2
        low, high = slice(0, n_far // 2), slice(n_far // 2, n_far)
        src, dst, t = (
            (remote_p.at[0, c], remote_p.at[1, c], tx),
            (remote_p.at[0, c], remote_p.at[2, c], ty),
            (remote_p.at[1, c, low], remote_p.at[3, c, low], ty),
            (remote_p.at[2, c, high], remote_p.at[3, c, high], tx),
        )[k]
        return remote(src, dst, ag_send.at[c, k], ag_recv.at[c, k], me_e, t)

    def arrive(c):
        for dz in z_order:
            z_copy(c, dz, 0).wait_recv()
            z_copy(c, dz, 1).wait_recv()
        ag_copy(c, 0).start()
        ag_copy(c, 1).start()

    def local_forward():
        local_copy(0).wait_recv()
        local_copy(2).start()
        local_copy(1).wait_recv()
        local_copy(3).start()

    def pieces_of(c, j):
        far = remote_p[j, c].reshape((n_expert - 2) * piece, LANES)
        return jnp.concatenate([local_p[j, 0, c], local_p[j, 1, c], far], axis=0)

    def to_slots(c, blocks):
        wide_in = jnp.concatenate([pieces_of(c, j) for j in blocks], axis=1)
        out = dot_nn(gather_mat[...], wide_in).astype(BF16)
        for i, j in enumerate(blocks):
            for q in range(PARTS):
                rows[c, j * block : (j + 1) * block, q * LANES : (q + 1) * LANES] = out[
                    q * block : (q + 1) * block, i * LANES : (i + 1) * LANES
                ]

    def forward(c):
        ag_copy(c, 0).wait_recv()
        ag_copy(c, 2).start()
        ag_copy(c, 1).wait_recv()
        ag_copy(c, 3).start()

    def wait_diagonal(c):
        ag_copy(c, 2).wait_recv()
        ag_copy(c, 3).wait_recv()

    def through_part(c):
        wait_diagonal(c)
        to_slots(c, range(4))

        def body(i, carry):
            at = pl.ds(pl.multiple_of(i * TILE, TILE), TILE)
            part = dot_nt(rows[c], down_w[at, c * CHUNK : (c + 1) * CHUNK])
            if c == 0:
                through[:, at] = part
            else:
                through[:, at] = through[:, at] + part
            return carry

        lax.fori_loop(0, hid // TILE, body, 0)

    def down_term(c):
        def body(i, carry):
            at = pl.ds(pl.multiple_of(i * TILE, TILE), TILE)
            to = pl.ds(pl.multiple_of(c * CHUNK + i * TILE, TILE), TILE)
            down_out_ref[0, :, to] = dot_nn(hidden_t[...], rows[c, :, at]).astype(BF16)
            return carry

        lax.fori_loop(0, CHUNK // TILE, body, 0)

    def coefficients():
        for copy in loads:
            copy.wait()

        def body(i, carry):
            at = pl.ds(pl.multiple_of(i * ROW_TILE, ROW_TILE), ROW_TILE)
            gate = gate_v[at, :].astype(F32)
            up = up_v[at, :].astype(F32)
            sig = lax.logistic(gate)
            silu = gate * sig
            coef_up[at, :] = silu
            coef_gate[at, :] = up * sig * (1.0 + gate * (1.0 - sig))
            grad_up[at, :] = (silu * up).astype(BF16)
            return carry

        lax.fori_loop(0, n_rows // ROW_TILE, body, 0)

        def turn(i, carry):
            at = pl.ds(pl.multiple_of(i * LANES, LANES), LANES)
            hidden_t[:, at] = grad_up[at, :].T
            return carry

        lax.fori_loop(0, n_rows // LANES, turn, 0)

    arrive(0)
    send_far(2)
    coefficients()
    local_forward()
    arrive(1)
    send_far(3)
    forward(0)
    arrive(2)
    send_far(4)
    forward(1)
    load_down.wait()
    local_copy(2).wait_recv()
    local_copy(3).wait_recv()
    through_part(0)
    arrive(3)
    forward(2)
    down_term(0)
    through_part(1)
    arrive(4)
    forward(3)
    down_term(1)
    through_part(2)
    load_gate.wait()
    load_up.wait()
    through_part(3)

    def grads(i, carry):
        at = pl.ds(pl.multiple_of(i * ROW_TILE, ROW_TILE), ROW_TILE)
        value = through[at, :]
        silu = coef_up[at, :]
        grad_gate[at, :] = (value * coef_gate[at, :]).astype(BF16)
        grad_up[at, :] = (value * silu).astype(BF16)
        prod = value * silu * up_v[at, :].astype(F32)
        total = prod[:, 0:LANES]
        for k in range(1, hid // LANES):
            total = total + prod[:, k * LANES : (k + 1) * LANES]
        row_sum[at, :] = total
        return carry

    def finish_block(j):
        last = n_chunk - 1
        to_slots(last, [j])
        span = slice(j * block, (j + 1) * block)

        def body(i, carry):
            at = pl.ds(pl.multiple_of(i * TILE, TILE), TILE)
            part = dot_nt(rows[last, span, :], down_w[at, last * CHUNK : (last + 1) * CHUNK])
            through[span, at] = through[span, at] + part
            return carry

        lax.fori_loop(0, hid // TILE, body, 0)
        per = block // ROW_TILE
        lax.fori_loop(j * per, (j + 1) * per, grads, 0)

    def first_copy(c, k):
        begin = ((block, tx), (3 * block, tx), (2 * block + half, ty), (3 * block + half, ty))[k]
        return remote(
            term.at[c, begin[0] : begin[0] + half], got_first.at[c, k],
            first_send.at[c, k], first_recv.at[c, k], me_e, begin[1],
        )

    def second_copy(c, k):
        return remote(
            sum_out.at[c, k], got_second.at[c, k],
            second_send.at[c, k], second_recv.at[c, k], me_e, (ty, tx)[k],
        )

    def rz_copy(c, d):
        dest = lax.rem(me_e + d, n_expert)
        return remote(
            ret.at[c, dest], back.at[c, me_e], rz_send.at[c, d], rz_recv.at[c, d], dest, me_t
        )

    def make_term(c):
        for n in range(CHUNK // TILE):
            at = slice(c * CHUNK + n * TILE, c * CHUNK + (n + 1) * TILE)

            def body(j, carry):
                span = pl.ds(pl.multiple_of(j * 2 * block, 2 * block), 2 * block)
                value = dot_nt(grad_gate[span, :], gate_w[at, :])
                value = value + dot_nt(grad_up[span, :], up_w[at, :])
                term[c, span, n * TILE : (n + 1) * TILE] = value.astype(BF16)
                return carry

            lax.fori_loop(0, 2, body, 0)
        for k in (0, 2, 1, 3):
            first_copy(c, k).start()

    def first_block(j):
        span = slice(j * block, (j + 1) * block)

        def body(i, carry):
            at = pl.ds(pl.multiple_of(i * TILE, TILE), TILE)
            value = dot_nt(grad_gate[span, :], gate_w[at, :])
            value = value + dot_nt(grad_up[span, :], up_w[at, :])
            term[0, span, at] = value.astype(BF16)
            return carry

        lax.fori_loop(0, CHUNK // TILE, body, 0)

    def add(a, b):
        return a.astype(F32) + b.astype(F32)

    def second_stage(c):
        for k in range(2):
            first_copy(c, k).wait_recv()
        sum_out[c, 0] = add(term[c, 2 * block : 2 * block + half], got_first[c, 1]).astype(BF16)
        second_copy(c, 0).start()
        for k in range(2, 4):
            first_copy(c, k).wait_recv()
        sum_out[c, 1] = add(term[c, block + half : 2 * block], got_first[c, 3]).astype(BF16)
        second_copy(c, 1).start()

    def send_home(c):
        second_copy(c, 0).wait_recv()
        second_copy(c, 1).wait_recv()
        low = add(term[c, 0:half], got_first[c, 0]) + got_second[c, 0].astype(F32)
        high = add(term[c, half:block], got_first[c, 2]) + got_second[c, 1].astype(F32)
        total = jnp.concatenate([low.astype(BF16), high.astype(BF16)], axis=0)
        stack = jnp.concatenate(
            [total[:, q * LANES : (q + 1) * LANES] for q in range(PARTS)], axis=0
        )
        out = dot_nn(spread_mat[...], stack).astype(BF16)
        ret[c] = out.reshape(n_expert, piece, LANES)
        for d in far_first:
            rz_copy(c, d).start()
        back[c, me_e] = ret[c, me_e]

    def finish(c):
        for d in far_first[::-1]:
            rz_copy(c, d).wait_recv()
        out = dot_nn(pick_back[...], back[c].reshape(n_expert * piece, LANES)).astype(BF16)
        for q in range(PARTS):
            tokens_ref[:, c * CHUNK + q * LANES : c * CHUNK + (q + 1) * LANES] = out[
                q * tok : (q + 1) * tok
            ]

    wide = score_part.shape[2]

    def sp_copy(j):
        return remote(
            score_part.at[j], score_got.at[j], sp_send.at[j], sp_recv.at[j], me_e, peers[j]
        )

    def sz_copy(d):
        dest = lax.rem(me_e + d, n_expert)
        return remote(
            score_tot, score_back.at[me_e], sz_send.at[d], sz_recv.at[d], dest, me_t
        )

    def send_scores():
        ones = jnp.ones((ROW_TILE, LANES), BF16)
        score_part[...] = jnp.zeros(score_part.shape, F32)
        for j in range(4):
            high, low = split_bf16(row_sum[j * block : (j + 1) * block, :])
            line = dot_nt(ones, high) + dot_nt(ones, low)
            score_part[j, :, 0:block] = line[0:8]
        for j in range(1, 4):
            sp_copy(j).start()

    def total_scores():
        for j in range(1, 4):
            sp_copy(j).wait_recv()
        score_tot[...] = (score_part[0] + score_got[1]) + (score_got[2] + score_got[3])
        for d in far_first:
            sz_copy(d).start()
        score_back[me_e] = score_tot[...]

    def finish_scores():
        for d in far_first:
            sz_copy(d).wait_recv()
        lane = iota((wide, tok), 0)
        pick = one_where(lane == me_e * cap + place)
        high, low = split_bf16(score_back[...].reshape(n_expert * 8, wide))
        mixed = dot_nn(high, pick) + dot_nn(low, pick)
        keep = iota((n_expert * 8, tok), 0) == routing * 8
        value = jnp.sum(jnp.where(keep, mixed, 0.0), axis=0, keepdims=True)
        score_out_ref[...] = (value / score).astype(BF16)

    finish_block(0)
    forward(n_chunk - 1)
    finish_block(1)
    first_block(1)
    first_copy(0, 0).start()
    finish_block(2)
    first_block(2)
    first_copy(0, 2).start()
    wait_diagonal(n_chunk - 1)
    finish_block(3)
    first_block(3)
    first_copy(0, 1).start()
    first_copy(0, 3).start()
    make_term(1)
    first_block(0)
    send_scores()
    second_stage(0)
    make_term(2)
    second_stage(1)
    send_home(0)
    make_term(3)
    second_stage(2)
    send_home(1)
    total_scores()
    make_term(4)
    second_stage(3)
    send_home(2)
    down_term(2)
    finish(0)
    second_stage(4)
    send_home(3)
    down_term(3)
    finish(1)
    send_home(4)
    down_term(4)
    finish_scores()
    finish(2)
    finish(3)
    finish(4)

    for c in range(n_chunk):
        for d in range(1, n_expert):
            z_copy(c, d // 2, d % 2).wait_send()
            rz_copy(c, d).wait_send()
        for k in range(4):
            ag_copy(c, k).wait_send()
            first_copy(c, k).wait_send()
        for k in range(2):
            second_copy(c, k).wait_send()
    for k in range(4):
        local_copy(k).wait_send()
    for j in range(1, 4):
        sp_copy(j).wait_send()
    for d in range(1, n_expert):
        sz_copy(d).wait_send()


def hand_over(tokens_ref, score_ref, down_ref, tokens_out, score_out, down_out, out_sem):
    n_part = out_sem.shape[0] - 2
    height = down_ref.shape[1] // n_part
    pairs = [
        (down_ref.at[0, i * height : (i + 1) * height],
         down_out.at[0, i * height : (i + 1) * height])
        for i in range(n_part)
    ]
    pairs += [(tokens_ref, tokens_out), (score_ref, score_out)]
    outs = [pltpu.make_async_copy(a, b, out_sem.at[i]) for i, (a, b) in enumerate(pairs)]
    for out in outs:
        out.start()
    for out in outs:
        out.wait()


def fused_local(grad_out, router_score, routing, gate_pre, up_pre, gate_weight, up_weight, down_weight):
    n_expert = lax.axis_size("expert")
    tok, width = grad_out.shape
    cap = tok // n_expert + tok // (4 * n_expert)
    block = n_expert * cap
    piece = PARTS * cap
    n_rows = gate_pre.shape[1]
    hid = gate_pre.shape[2]
    n_chunk = width // CHUNK
    wide = -(-block // LANES) * LANES
    vmem = pl.BlockSpec(memory_space=pltpu.VMEM)
    hbm = pl.BlockSpec(memory_space=pl.ANY)
    dma = pltpu.SemaphoreType.DMA
    macs = 4 * n_rows * width * hid
    tokens, score, down = pl.pallas_call(
        functools.partial(kernel, n_expert, cap, n_chunk),
        out_shape=(
            pltpu.VMEM((tok, width), BF16),
            pltpu.VMEM((1, tok), BF16),
            pltpu.VMEM((1, hid, width), BF16),
        ),
        in_specs=[vmem, vmem, vmem, hbm, hbm, hbm, hbm, hbm],
        out_specs=(vmem, vmem, vmem),
        scratch_shapes=[
            pltpu.VMEM((width, hid), BF16),
            pltpu.VMEM((width, hid), BF16),
            pltpu.VMEM((hid, width), BF16),
            pltpu.VMEM((n_rows, hid), BF16),
            pltpu.VMEM((n_rows, hid), BF16),
            pltpu.VMEM((n_rows, hid), F32),
            pltpu.VMEM((n_rows, hid), F32),
            pltpu.VMEM((hid, n_rows), BF16),
            pltpu.VMEM((n_rows, hid), F32),
            pltpu.VMEM((n_rows, hid), BF16),
            pltpu.VMEM((n_rows, hid), BF16),
            pltpu.VMEM((n_expert * piece, PARTS * tok), BF16),
            pltpu.VMEM((PARTS * tok, n_expert * piece), BF16),
            pltpu.VMEM((PARTS * block, n_expert * piece), BF16),
            pltpu.VMEM((n_expert * piece, PARTS * block), BF16),
            pltpu.VMEM((n_chunk, n_expert, piece, LANES), BF16),
            pltpu.VMEM((4, 2, n_chunk, piece, LANES), BF16),
            pltpu.VMEM((4, n_chunk, n_expert - 2, piece, LANES), BF16),
            pltpu.VMEM((n_chunk, n_rows, CHUNK), BF16),
            pltpu.VMEM((n_chunk, n_rows, CHUNK), BF16),
            pltpu.VMEM((n_chunk, 4, block // 2, CHUNK), BF16),
            pltpu.VMEM((n_chunk, 2, block // 2, CHUNK), BF16),
            pltpu.VMEM((n_chunk, 2, block // 2, CHUNK), BF16),
            pltpu.VMEM((n_chunk, n_expert, piece, LANES), BF16),
            pltpu.VMEM((n_chunk, n_expert, piece, LANES), BF16),
            pltpu.VMEM((n_rows, LANES), F32),
            pltpu.VMEM((4, 8, wide), F32),
            pltpu.VMEM((4, 8, wide), F32),
            pltpu.VMEM((8, wide), F32),
            pltpu.VMEM((n_expert, 8, wide), F32),
            dma((n_chunk, n_expert)),
            dma((n_chunk, n_expert)),
            dma((4,)),
            dma((4,)),
            dma((n_chunk, 4)),
            dma((n_chunk, 4)),
            dma((n_chunk, 4)),
            dma((n_chunk, 4)),
            dma((n_chunk, 2)),
            dma((n_chunk, 2)),
            dma((n_chunk, n_expert)),
            dma((n_chunk, n_expert)),
            dma((4,)),
            dma((4,)),
            dma((n_expert,)),
            dma((n_expert,)),
            dma((11,)),
        ],
        compiler_params=pltpu.CompilerParams(
            collective_id=0, has_side_effects=True, vmem_limit_bytes=54 * 1024 * 1024
        ),
        cost_estimate=pl.CostEstimate(
            flops=2 * macs,
            bytes_accessed=2 * (4 * width * hid + 2 * n_rows * hid),
            transcendentals=n_rows * hid,
        ),
        name="routed_backward",
    )(
        grad_out,
        router_score.reshape(1, tok),
        routing.reshape(1, tok),
        gate_pre,
        up_pre,
        gate_weight,
        up_weight,
        down_weight,
    )
    n_part = 4
    tokens, score, down = pl.pallas_call(
        hand_over,
        out_shape=(
            jax.ShapeDtypeStruct((tok, width), BF16),
            jax.ShapeDtypeStruct((1, tok), BF16),
            jax.ShapeDtypeStruct((1, hid, width), BF16),
        ),
        in_specs=[vmem, vmem, vmem],
        out_specs=(hbm, hbm, hbm),
        scratch_shapes=[dma((n_part + 2,))],
        compiler_params=pltpu.CompilerParams(vmem_limit_bytes=1024 * 1024),
        name="hand_over",
    )(tokens, score, down)
    return tokens, score.reshape(tok), down


def fits(mesh, grad_out, gate_pre):
    n_expert, n_tensor = mesh.shape["expert"], mesh.shape["tensor"]
    tok = grad_out.shape[0] // (n_expert * n_tensor)
    cap = tok // n_expert + tok // (4 * n_expert)
    return (
        n_tensor == 4
        and n_expert <= ROW_TILE
        and n_expert % 2 == 0
        and n_expert >= 4
        and cap % 4 == 0
        and (n_expert * cap) % 32 == 0
        and tok % LANES == 0
        and grad_out.shape[1] == 5 * CHUNK
        and gate_pre.shape[2] % (256 * n_tensor) == 0
    )


def expert_rows(rows_grad, rows_score, gate_rows, up_rows, down_local):
    through = lax.dot_general(
        rows_grad, down_local, (((1,), (1,)), ((), ())), preferred_element_type=jnp.float32
    )
    gate_val = gate_rows.astype(jnp.float32)
    up_val = up_rows.astype(jnp.float32)
    sig_gate = jax.nn.sigmoid(gate_val)
    hidden = gate_val * sig_gate * up_val
    part_score = jnp.sum(through * hidden, axis=1)
    scale_col = rows_score.astype(jnp.float32)[:, None]
    scaled = scale_col * through
    grad_gate = (scaled * up_val * sig_gate * (1.0 + gate_val * (1.0 - sig_gate))).astype(
        jnp.bfloat16
    )
    grad_up = (scaled * gate_val * sig_gate).astype(jnp.bfloat16)
    weighted = (scale_col * hidden).astype(jnp.bfloat16)
    down_term = lax.dot_general(
        weighted, rows_grad, (((0,), (0,)), ((), ())), preferred_element_type=jnp.float32
    )
    return (grad_gate, grad_up, part_score, down_term)


def local(grad_out, router_score, routing, gate_pre, up_pre, gate_weight, up_weight, down_weight):
    n_expert = lax.axis_size("expert")
    tok_count = grad_out.shape[0]
    width = grad_out.shape[1]
    capacity = tok_count // n_expert + tok_count // (4 * n_expert)
    slot_count = n_expert * capacity
    gate_local = gate_pre[0]
    up_local = up_pre[0]
    down_local = down_weight[0]
    gate_mat = gate_weight[0]
    up_mat = up_weight[0]
    expert_ids = routing[:, 0]
    onehot = (expert_ids[:, None] == jnp.arange(n_expert, dtype=jnp.int32)[None, :]).astype(
        jnp.int32
    )
    before = jnp.cumsum(onehot, axis=0) - onehot
    position = jnp.sum(before * onehot, axis=1)
    slot_index = expert_ids * capacity + position
    send_grad = jnp.zeros((slot_count, width), jnp.bfloat16).at[slot_index].set(grad_out)
    send_score = jnp.zeros((slot_count,), jnp.bfloat16).at[slot_index].set(router_score)
    recv_grad, recv_score = (
        lax.all_to_all(
            send_grad.reshape(n_expert, capacity, width),
            "expert",
            split_axis=0,
            concat_axis=0,
            tiled=True,
        ),
        lax.all_to_all(
            send_score.reshape(n_expert, capacity),
            "expert",
            split_axis=0,
            concat_axis=0,
            tiled=True,
        ),
    )
    recv_grad = recv_grad.reshape(slot_count, width)
    recv_score = recv_score.reshape(slot_count)
    all_grad, all_score = (
        lax.all_gather(recv_grad, "tensor", axis=0, tiled=True),
        lax.all_gather(recv_score, "tensor", axis=0, tiled=True),
    )
    grad_gate, grad_up, part_score, down_sum = expert_rows(
        all_grad, all_score, gate_local, up_local, down_local
    )
    term = lax.dot_general(
        grad_gate, gate_mat, (((1,), (1,)), ((), ())), preferred_element_type=jnp.float32
    )
    mine_grad = lax.psum_scatter(
        (
            term
            + lax.dot_general(
                grad_up, up_mat, (((1,), (1,)), ((), ())), preferred_element_type=jnp.float32
            )
        ).astype(jnp.bfloat16),
        "tensor",
        scatter_dimension=0,
        tiled=True,
    )
    mine_score = lax.psum_scatter(part_score, "tensor", scatter_dimension=0, tiled=True)
    back_grad, back_score = (
        lax.all_to_all(
            mine_grad.reshape(n_expert, capacity, width),
            "expert",
            split_axis=0,
            concat_axis=0,
            tiled=True,
        ),
        lax.all_to_all(
            mine_score.astype(jnp.bfloat16).reshape(n_expert, capacity),
            "expert",
            split_axis=0,
            concat_axis=0,
            tiled=True,
        ),
    )
    grad_tokens = back_grad.reshape(slot_count, width)[slot_index]
    grad_score = back_score.reshape(slot_count)[slot_index]
    grad_down_weight = down_sum.astype(jnp.bfloat16)[None]
    return (grad_tokens, grad_score, grad_down_weight)


def solution(mesh):
    def run(*arrays):
        body = fused_local if fits(mesh, arrays[0], arrays[3]) else local
        return jax.shard_map(
            body,
            mesh=mesh,
            in_specs=(
                P(("expert", "tensor"), None),
                P(("expert", "tensor")),
                P(("expert", "tensor"), None),
                P("expert", None, "tensor"),
                P("expert", None, "tensor"),
                P("expert", None, "tensor"),
                P("expert", None, "tensor"),
                P("expert", "tensor", None),
            ),
            out_specs=(
                P(("expert", "tensor"), None),
                P(("expert", "tensor")),
                P("expert", "tensor", None),
            ),
            check_vma=False,
        )(*arrays)

    return run
```

```python
import functools

import jax
import jax.numpy as jnp
from jax import lax
from jax.experimental import pallas as pl
from jax.experimental.pallas import tpu as pltpu
from jax.sharding import PartitionSpec as P

MESH = pl.DeviceIdType.MESH
LANES = 128
PARTS = 4
CHUNK = PARTS * LANES
ROW_TILE = 16
TILE = 256
F32 = jnp.float32
BF16 = jnp.bfloat16


def dot_nn(a, b):
    return lax.dot_general(a, b, (((1,), (0,)), ((), ())), preferred_element_type=F32)


def dot_nt(a, b):
    return lax.dot_general(a, b, (((1,), (1,)), ((), ())), preferred_element_type=F32)


def dot_tn(a, b):
    return lax.dot_general(a, b, (((0,), (0,)), ((), ())), preferred_element_type=F32)


def split_bf16(value):
    high = value.astype(BF16)
    return high, (value - high.astype(F32)).astype(BF16)


def iota(shape, dim):
    return lax.broadcasted_iota(jnp.int32, shape, dim)


def one_where(mask):
    return jnp.where(mask, 1.0, 0.0).astype(BF16)


def kernel(
    n_expert, cap, n_chunk,
    grad_ref, score_ref, routing_ref, gate_pre_ref, up_pre_ref, gate_w_ref, up_w_ref, down_w_ref,
    tokens_ref, score_out_ref, down_out_ref,
    gate_w, up_w, down_w, gate_v, up_v, coef_gate, coef_up, hidden_t, through, grad_gate, grad_up,
    pick_send, pick_back, gather_mat, spread_mat,
    send, local_p, remote_p, rows, term, got_first, sum_out, got_second, ret, back,
    row_sum, score_part, score_got, score_tot, score_back,
    z_send, z_recv, lg_send, lg_recv, ag_send, ag_recv, first_send, first_recv, second_send, second_recv,
    rz_send, rz_recv, sp_send, sp_recv, sz_send, sz_recv, load_sem,
):
    tok = grad_ref.shape[0]
    block = n_expert * cap
    half = block // 2
    piece = PARTS * cap
    n_rows = PARTS * block
    hid = gate_v.shape[1]
    me_e = lax.axis_index("expert")
    me_t = lax.axis_index("tensor")
    near = me_t + 1 - 2 * lax.rem(me_t, 2)
    over = lax.rem(me_t + 2, 4)
    td = 3 - me_t
    odd = lax.rem(me_e, 2)
    tx = near + odd * (over - near)
    ty = over + odd * (near - over)
    peers = (me_t, tx, ty, td)

    barrier = pltpu.get_barrier_semaphore()
    for d in range(1, n_expert):
        pl.semaphore_signal(
            barrier, inc=1, device_id=(lax.rem(me_e + d, n_expert), me_t), device_id_type=MESH
        )
    for j in range(1, 4):
        pl.semaphore_signal(barrier, inc=1, device_id=(me_e, peers[j]), device_id_type=MESH)

    loads = []
    for j in range(4):
        start = pl.multiple_of(peers[j] * block, block)
        for k, (src, dst) in enumerate(((gate_pre_ref, gate_v), (up_pre_ref, up_v))):
            loads.append(
                pltpu.make_async_copy(
                    src.at[0, pl.ds(start, block)],
                    dst.at[pl.ds(j * block, block)],
                    load_sem.at[2 * j + k],
                )
            )
    load_down = pltpu.make_async_copy(down_w_ref.at[0], down_w, load_sem.at[8])
    load_gate = pltpu.make_async_copy(gate_w_ref.at[0], gate_w, load_sem.at[9])
    load_up = pltpu.make_async_copy(up_w_ref.at[0], up_w, load_sem.at[10])
    for copy in loads + [load_down, load_gate, load_up]:
        copy.start()

    def remote(src, dst, s_sem, r_sem, e, t):
        return pltpu.make_async_remote_copy(
            src_ref=src, dst_ref=dst, send_sem=s_sem, recv_sem=r_sem,
            device_id=(e, t), device_id_type=MESH,
        )

    routing = routing_ref[...]
    named = iota((ROW_TILE, tok), 0) == routing
    earlier = one_where(iota((tok, tok), 0) < iota((tok, tok), 1))
    before = dot_nn(one_where(named), earlier)
    place = jnp.sum(jnp.where(named, before, 0.0), axis=0, keepdims=True).astype(jnp.int32)
    key = routing * piece + place
    score = score_ref[...].astype(F32)
    spot = iota((n_expert * piece, tok), 0)
    for q in range(PARTS):
        pick_send[:, q * tok : (q + 1) * tok] = jnp.where(
            spot == key + q * cap, score, 0.0
        ).astype(BF16)

    plane = me_e // 2
    core = lax.rem(me_e, 2)
    n_plane = n_expert // 2

    def z_copy(c, dz, dc):
        dest = lax.rem(plane + dz, n_plane) * 2 + lax.rem(core + dc, 2)
        seen = (n_plane - dz) % n_plane
        if dz == 0:
            landing = local_p.at[0, core, c]
        else:
            landing = remote_p.at[0, c, (seen - 1) * 2 + core]
        return remote(
            send.at[c, dest], landing, z_send.at[c, 2 * dz + dc], z_recv.at[c, 2 * seen + dc],
            dest, me_t,
        )

    far_first = sorted(range(1, n_expert), key=lambda d: -min(d, n_expert - d))
    z_order = sorted(range(1, n_plane), key=lambda d: -min(d, n_plane - d))

    def dispatch(c):
        stack = jnp.concatenate(
            [
                grad_ref[:, c * CHUNK + q * LANES : c * CHUNK + (q + 1) * LANES]
                for q in range(PARTS)
            ],
            axis=0,
        )
        out = dot_nn(pick_send[...], stack).astype(BF16)
        send[c] = out.reshape(n_expert, piece, LANES)
        if c == 0:
            pl.semaphore_wait(barrier, n_expert - 1 + 3)
        z_copy(c, 0, 1).start()
        local_p[0, core, c] = send[c, me_e]

    def send_far(c):
        for dz in z_order:
            z_copy(c, dz, 0).start()
            z_copy(c, dz, 1).start()

    def local_copy(k):
        src, dst, t = (
            (local_p.at[0], local_p.at[1], tx),
            (local_p.at[0], local_p.at[2], ty),
            (local_p.at[1, 0], local_p.at[3, 0], ty),
            (local_p.at[2, 1], local_p.at[3, 1], tx),
        )[k]
        return remote(src, dst, lg_send.at[k], lg_recv.at[k], me_e, t)

    dispatch(0)
    send_far(0)
    dispatch(1)
    send_far(1)
    for c in range(2, n_chunk):
        dispatch(c)
    for c in range(n_chunk):
        z_copy(c, 0, 1).wait_recv()
    local_copy(0).start()
    local_copy(1).start()

    key_f = key.astype(F32)
    key_col = jnp.sum(
        jnp.where(iota((tok, tok), 0) == iota((tok, tok), 1), key_f, 0.0), axis=1, keepdims=True
    ).astype(jnp.int32)
    lane_spot = iota((tok, n_expert * piece), 1)
    for q in range(PARTS):
        pick_back[q * tok : (q + 1) * tok, :] = one_where(lane_spot == key_col + q * cap)
    for q in range(PARTS):
        r = iota((block, n_expert * piece), 0)
        s = sum((r >= k * cap).astype(jnp.int32) for k in range(1, n_expert))
        lane = iota((block, n_expert * piece), 1)
        at = slice(q * block, (q + 1) * block)
        spot_abs = r + s * (piece - cap) + q * cap
        spread_t = one_where(lane == spot_abs)
        shift = spot_abs - 2 * piece * plane
        shift = jnp.where(shift < 0, shift + n_expert * piece, shift)
        spread_mat[:, at] = spread_t.T
        gather_mat[at, :] = one_where(lane == shift)

    def ag_copy(c, k):
        n_far = n_expert - 2
        low, high = slice(0, n_far // 2), slice(n_far // 2, n_far)
        src, dst, t = (
            (remote_p.at[0, c], remote_p.at[1, c], tx),
            (remote_p.at[0, c], remote_p.at[2, c], ty),
            (remote_p.at[1, c, low], remote_p.at[3, c, low], ty),
            (remote_p.at[2, c, high], remote_p.at[3, c, high], tx),
        )[k]
        return remote(src, dst, ag_send.at[c, k], ag_recv.at[c, k], me_e, t)

    def arrive(c):
        for dz in z_order:
            z_copy(c, dz, 0).wait_recv()
            z_copy(c, dz, 1).wait_recv()
        ag_copy(c, 0).start()
        ag_copy(c, 1).start()

    def local_forward():
        local_copy(0).wait_recv()
        local_copy(2).start()
        local_copy(1).wait_recv()
        local_copy(3).start()

    def pieces_of(c, j):
        far = remote_p[j, c].reshape((n_expert - 2) * piece, LANES)
        return jnp.concatenate([local_p[j, 0, c], local_p[j, 1, c], far], axis=0)

    def to_slots(c, blocks):
        wide_in = jnp.concatenate([pieces_of(c, j) for j in blocks], axis=1)
        out = dot_nn(gather_mat[...], wide_in).astype(BF16)
        for i, j in enumerate(blocks):
            for q in range(PARTS):
                rows[c, j * block : (j + 1) * block, q * LANES : (q + 1) * LANES] = out[
                    q * block : (q + 1) * block, i * LANES : (i + 1) * LANES
                ]

    def forward(c):
        ag_copy(c, 0).wait_recv()
        ag_copy(c, 2).start()
        ag_copy(c, 1).wait_recv()
        ag_copy(c, 3).start()

    def wait_diagonal(c):
        ag_copy(c, 2).wait_recv()
        ag_copy(c, 3).wait_recv()

    def through_part(c):
        wait_diagonal(c)
        to_slots(c, range(4))

        def body(i, carry):
            at = pl.ds(pl.multiple_of(i * TILE, TILE), TILE)
            part = dot_nt(rows[c], down_w[at, c * CHUNK : (c + 1) * CHUNK])
            if c == 0:
                through[:, at] = part
            else:
                through[:, at] = through[:, at] + part
            return carry

        lax.fori_loop(0, hid // TILE, body, 0)

    def down_term(c):
        def body(i, carry):
            at = pl.ds(pl.multiple_of(i * TILE, TILE), TILE)
            to = pl.ds(pl.multiple_of(c * CHUNK + i * TILE, TILE), TILE)
            down_out_ref[0, :, to] = dot_nn(hidden_t[...], rows[c, :, at]).astype(BF16)
            return carry

        lax.fori_loop(0, CHUNK // TILE, body, 0)

    def coefficients():
        for copy in loads:
            copy.wait()

        def body(i, carry):
            at = pl.ds(pl.multiple_of(i * ROW_TILE, ROW_TILE), ROW_TILE)
            gate = gate_v[at, :].astype(F32)
            up = up_v[at, :].astype(F32)
            sig = lax.logistic(gate)
            silu = gate * sig
            coef_up[at, :] = silu
            coef_gate[at, :] = up * sig * (1.0 + gate * (1.0 - sig))
            grad_up[at, :] = (silu * up).astype(BF16)
            return carry

        lax.fori_loop(0, n_rows // ROW_TILE, body, 0)

        def turn(i, carry):
            at = pl.ds(pl.multiple_of(i * LANES, LANES), LANES)
            hidden_t[:, at] = grad_up[at, :].T
            return carry

        lax.fori_loop(0, n_rows // LANES, turn, 0)

    arrive(0)
    send_far(2)
    coefficients()
    local_forward()
    arrive(1)
    send_far(3)
    forward(0)
    arrive(2)
    send_far(4)
    forward(1)
    load_down.wait()
    local_copy(2).wait_recv()
    local_copy(3).wait_recv()
    through_part(0)
    arrive(3)
    forward(2)
    down_term(0)
    through_part(1)
    arrive(4)
    forward(3)
    through_part(2)
    forward(n_chunk - 1)
    load_gate.wait()
    load_up.wait()
    through_part(3)

    def grads(i, carry):
        at = pl.ds(pl.multiple_of(i * ROW_TILE, ROW_TILE), ROW_TILE)
        value = through[at, :]
        silu = coef_up[at, :]
        grad_gate[at, :] = (value * coef_gate[at, :]).astype(BF16)
        grad_up[at, :] = (value * silu).astype(BF16)
        prod = value * silu * up_v[at, :].astype(F32)
        total = prod[:, 0:LANES]
        for k in range(1, hid // LANES):
            total = total + prod[:, k * LANES : (k + 1) * LANES]
        row_sum[at, :] = total
        return carry

    def finish_block(j):
        last = n_chunk - 1
        to_slots(last, [j])
        span = slice(j * block, (j + 1) * block)

        def body(i, carry):
            at = pl.ds(pl.multiple_of(i * TILE, TILE), TILE)
            part = dot_nt(rows[last, span, :], down_w[at, last * CHUNK : (last + 1) * CHUNK])
            through[span, at] = through[span, at] + part
            return carry

        lax.fori_loop(0, hid // TILE, body, 0)
        per = block // ROW_TILE
        lax.fori_loop(j * per, (j + 1) * per, grads, 0)

    def first_copy(c, k):
        begin = ((block, tx), (3 * block, tx), (2 * block + half, ty), (3 * block + half, ty))[k]
        return remote(
            term.at[c, begin[0] : begin[0] + half], got_first.at[c, k],
            first_send.at[c, k], first_recv.at[c, k], me_e, begin[1],
        )

    def second_copy(c, k):
        return remote(
            sum_out.at[c, k], got_second.at[c, k],
            second_send.at[c, k], second_recv.at[c, k], me_e, (ty, tx)[k],
        )

    def rz_copy(c, d):
        dest = lax.rem(me_e + d, n_expert)
        return remote(
            ret.at[c, dest], back.at[c, me_e], rz_send.at[c, d], rz_recv.at[c, d], dest, me_t
        )

    def make_term(c):
        for n in range(CHUNK // TILE):
            at = slice(c * CHUNK + n * TILE, c * CHUNK + (n + 1) * TILE)

            def body(j, carry):
                span = pl.ds(pl.multiple_of(j * 2 * block, 2 * block), 2 * block)
                value = dot_nt(grad_gate[span, :], gate_w[at, :])
                value = value + dot_nt(grad_up[span, :], up_w[at, :])
                term[c, span, n * TILE : (n + 1) * TILE] = value.astype(BF16)
                return carry

            lax.fori_loop(0, 2, body, 0)
        for k in (0, 2, 1, 3):
            first_copy(c, k).start()

    def first_block(j):
        span = slice(j * block, (j + 1) * block)

        def body(i, carry):
            at = pl.ds(pl.multiple_of(i * TILE, TILE), TILE)
            value = dot_nt(grad_gate[span, :], gate_w[at, :])
            value = value + dot_nt(grad_up[span, :], up_w[at, :])
            term[0, span, at] = value.astype(BF16)
            return carry

        lax.fori_loop(0, CHUNK // TILE, body, 0)

    def add(a, b):
        return a.astype(F32) + b.astype(F32)

    def second_stage(c):
        for k in range(2):
            first_copy(c, k).wait_recv()
        sum_out[c, 0] = add(term[c, 2 * block : 2 * block + half], got_first[c, 1]).astype(BF16)
        second_copy(c, 0).start()
        for k in range(2, 4):
            first_copy(c, k).wait_recv()
        sum_out[c, 1] = add(term[c, block + half : 2 * block], got_first[c, 3]).astype(BF16)
        second_copy(c, 1).start()

    def send_home(c):
        second_copy(c, 0).wait_recv()
        second_copy(c, 1).wait_recv()
        low = add(term[c, 0:half], got_first[c, 0]) + got_second[c, 0].astype(F32)
        high = add(term[c, half:block], got_first[c, 2]) + got_second[c, 1].astype(F32)
        total = jnp.concatenate([low.astype(BF16), high.astype(BF16)], axis=0)
        stack = jnp.concatenate(
            [total[:, q * LANES : (q + 1) * LANES] for q in range(PARTS)], axis=0
        )
        out = dot_nn(spread_mat[...], stack).astype(BF16)
        ret[c] = out.reshape(n_expert, piece, LANES)
        for d in far_first:
            rz_copy(c, d).start()
        back[c, me_e] = ret[c, me_e]

    def finish(c):
        for d in far_first[::-1]:
            rz_copy(c, d).wait_recv()
        out = dot_nn(pick_back[...], back[c].reshape(n_expert * piece, LANES)).astype(BF16)
        for q in range(PARTS):
            tokens_ref[:, c * CHUNK + q * LANES : c * CHUNK + (q + 1) * LANES] = out[
                q * tok : (q + 1) * tok
            ]

    wide = score_part.shape[2]

    def sp_copy(j):
        return remote(
            score_part.at[j], score_got.at[j], sp_send.at[j], sp_recv.at[j], me_e, peers[j]
        )

    def sz_copy(d):
        dest = lax.rem(me_e + d, n_expert)
        return remote(
            score_tot, score_back.at[me_e], sz_send.at[d], sz_recv.at[d], dest, me_t
        )

    def send_scores():
        ones = jnp.ones((ROW_TILE, LANES), BF16)
        score_part[...] = jnp.zeros(score_part.shape, F32)
        for j in range(4):
            high, low = split_bf16(row_sum[j * block : (j + 1) * block, :])
            line = dot_nt(ones, high) + dot_nt(ones, low)
            score_part[j, :, 0:block] = line[0:8]
        for j in range(1, 4):
            sp_copy(j).start()

    def total_scores():
        for j in range(1, 4):
            sp_copy(j).wait_recv()
        score_tot[...] = (score_part[0] + score_got[1]) + (score_got[2] + score_got[3])
        for d in far_first:
            sz_copy(d).start()
        score_back[me_e] = score_tot[...]

    def finish_scores():
        for d in far_first:
            sz_copy(d).wait_recv()
        lane = iota((wide, tok), 0)
        pick = one_where(lane == me_e * cap + place)
        high, low = split_bf16(score_back[...].reshape(n_expert * 8, wide))
        mixed = dot_nn(high, pick) + dot_nn(low, pick)
        keep = iota((n_expert * 8, tok), 0) == routing * 8
        value = jnp.sum(jnp.where(keep, mixed, 0.0), axis=0, keepdims=True)
        score_out_ref[...] = (value / score).astype(BF16)

    finish_block(0)
    finish_block(1)
    first_block(1)
    first_copy(0, 0).start()
    finish_block(2)
    first_block(2)
    first_copy(0, 2).start()
    wait_diagonal(n_chunk - 1)
    finish_block(3)
    first_block(3)
    first_copy(0, 1).start()
    first_copy(0, 3).start()
    make_term(1)
    first_block(0)
    send_scores()
    second_stage(0)
    make_term(2)
    second_stage(1)
    send_home(0)
    make_term(3)
    second_stage(2)
    send_home(1)
    down_term(1)
    total_scores()
    make_term(4)
    second_stage(3)
    send_home(2)
    down_term(2)
    finish(0)
    second_stage(4)
    send_home(3)
    down_term(3)
    finish(1)
    send_home(4)
    down_term(4)
    finish_scores()
    finish(2)
    finish(3)
    finish(4)

    for c in range(n_chunk):
        for d in range(1, n_expert):
            z_copy(c, d // 2, d % 2).wait_send()
            rz_copy(c, d).wait_send()
        for k in range(4):
            ag_copy(c, k).wait_send()
            first_copy(c, k).wait_send()
        for k in range(2):
            second_copy(c, k).wait_send()
    for k in range(4):
        local_copy(k).wait_send()
    for j in range(1, 4):
        sp_copy(j).wait_send()
    for d in range(1, n_expert):
        sz_copy(d).wait_send()


def hand_over(tokens_ref, score_ref, down_ref, tokens_out, score_out, down_out, out_sem):
    n_part = out_sem.shape[0] - 2
    height = down_ref.shape[1] // n_part
    pairs = [
        (down_ref.at[0, i * height : (i + 1) * height],
         down_out.at[0, i * height : (i + 1) * height])
        for i in range(n_part)
    ]
    pairs += [(tokens_ref, tokens_out), (score_ref, score_out)]
    outs = [pltpu.make_async_copy(a, b, out_sem.at[i]) for i, (a, b) in enumerate(pairs)]
    for out in outs:
        out.start()
    for out in outs:
        out.wait()


def fused_local(grad_out, router_score, routing, gate_pre, up_pre, gate_weight, up_weight, down_weight):
    n_expert = lax.axis_size("expert")
    tok, width = grad_out.shape
    cap = tok // n_expert + tok // (4 * n_expert)
    block = n_expert * cap
    piece = PARTS * cap
    n_rows = gate_pre.shape[1]
    hid = gate_pre.shape[2]
    n_chunk = width // CHUNK
    wide = -(-block // LANES) * LANES
    vmem = pl.BlockSpec(memory_space=pltpu.VMEM)
    hbm = pl.BlockSpec(memory_space=pl.ANY)
    dma = pltpu.SemaphoreType.DMA
    macs = 4 * n_rows * width * hid
    tokens, score, down = pl.pallas_call(
        functools.partial(kernel, n_expert, cap, n_chunk),
        out_shape=(
            pltpu.VMEM((tok, width), BF16),
            pltpu.VMEM((1, tok), BF16),
            pltpu.VMEM((1, hid, width), BF16),
        ),
        in_specs=[vmem, vmem, vmem, hbm, hbm, hbm, hbm, hbm],
        out_specs=(vmem, vmem, vmem),
        scratch_shapes=[
            pltpu.VMEM((width, hid), BF16),
            pltpu.VMEM((width, hid), BF16),
            pltpu.VMEM((hid, width), BF16),
            pltpu.VMEM((n_rows, hid), BF16),
            pltpu.VMEM((n_rows, hid), BF16),
            pltpu.VMEM((n_rows, hid), F32),
            pltpu.VMEM((n_rows, hid), F32),
            pltpu.VMEM((hid, n_rows), BF16),
            pltpu.VMEM((n_rows, hid), F32),
            pltpu.VMEM((n_rows, hid), BF16),
            pltpu.VMEM((n_rows, hid), BF16),
            pltpu.VMEM((n_expert * piece, PARTS * tok), BF16),
            pltpu.VMEM((PARTS * tok, n_expert * piece), BF16),
            pltpu.VMEM((PARTS * block, n_expert * piece), BF16),
            pltpu.VMEM((n_expert * piece, PARTS * block), BF16),
            pltpu.VMEM((n_chunk, n_expert, piece, LANES), BF16),
            pltpu.VMEM((4, 2, n_chunk, piece, LANES), BF16),
            pltpu.VMEM((4, n_chunk, n_expert - 2, piece, LANES), BF16),
            pltpu.VMEM((n_chunk, n_rows, CHUNK), BF16),
            pltpu.VMEM((n_chunk, n_rows, CHUNK), BF16),
            pltpu.VMEM((n_chunk, 4, block // 2, CHUNK), BF16),
            pltpu.VMEM((n_chunk, 2, block // 2, CHUNK), BF16),
            pltpu.VMEM((n_chunk, 2, block // 2, CHUNK), BF16),
            pltpu.VMEM((n_chunk, n_expert, piece, LANES), BF16),
            pltpu.VMEM((n_chunk, n_expert, piece, LANES), BF16),
            pltpu.VMEM((n_rows, LANES), F32),
            pltpu.VMEM((4, 8, wide), F32),
            pltpu.VMEM((4, 8, wide), F32),
            pltpu.VMEM((8, wide), F32),
            pltpu.VMEM((n_expert, 8, wide), F32),
            dma((n_chunk, n_expert)),
            dma((n_chunk, n_expert)),
            dma((4,)),
            dma((4,)),
            dma((n_chunk, 4)),
            dma((n_chunk, 4)),
            dma((n_chunk, 4)),
            dma((n_chunk, 4)),
            dma((n_chunk, 2)),
            dma((n_chunk, 2)),
            dma((n_chunk, n_expert)),
            dma((n_chunk, n_expert)),
            dma((4,)),
            dma((4,)),
            dma((n_expert,)),
            dma((n_expert,)),
            dma((11,)),
        ],
        compiler_params=pltpu.CompilerParams(
            collective_id=0, has_side_effects=True, vmem_limit_bytes=54 * 1024 * 1024
        ),
        cost_estimate=pl.CostEstimate(
            flops=2 * macs,
            bytes_accessed=2 * (4 * width * hid + 2 * n_rows * hid),
            transcendentals=n_rows * hid,
        ),
        name="routed_backward",
    )(
        grad_out,
        router_score.reshape(1, tok),
        routing.reshape(1, tok),
        gate_pre,
        up_pre,
        gate_weight,
        up_weight,
        down_weight,
    )
    n_part = 4
    tokens, score, down = pl.pallas_call(
        hand_over,
        out_shape=(
            jax.ShapeDtypeStruct((tok, width), BF16),
            jax.ShapeDtypeStruct((1, tok), BF16),
            jax.ShapeDtypeStruct((1, hid, width), BF16),
        ),
        in_specs=[vmem, vmem, vmem],
        out_specs=(hbm, hbm, hbm),
        scratch_shapes=[dma((n_part + 2,))],
        compiler_params=pltpu.CompilerParams(vmem_limit_bytes=1024 * 1024),
        name="hand_over",
    )(tokens, score, down)
    return tokens, score.reshape(tok), down


def fits(mesh, grad_out, gate_pre):
    n_expert, n_tensor = mesh.shape["expert"], mesh.shape["tensor"]
    tok = grad_out.shape[0] // (n_expert * n_tensor)
    cap = tok // n_expert + tok // (4 * n_expert)
    return (
        n_tensor == 4
        and n_expert <= ROW_TILE
        and n_expert % 2 == 0
        and n_expert >= 4
        and cap % 4 == 0
        and (n_expert * cap) % 32 == 0
        and tok % LANES == 0
        and grad_out.shape[1] == 5 * CHUNK
        and gate_pre.shape[2] % (256 * n_tensor) == 0
    )


def expert_rows(rows_grad, rows_score, gate_rows, up_rows, down_local):
    through = lax.dot_general(
        rows_grad, down_local, (((1,), (1,)), ((), ())), preferred_element_type=jnp.float32
    )
    gate_val = gate_rows.astype(jnp.float32)
    up_val = up_rows.astype(jnp.float32)
    sig_gate = jax.nn.sigmoid(gate_val)
    hidden = gate_val * sig_gate * up_val
    part_score = jnp.sum(through * hidden, axis=1)
    scale_col = rows_score.astype(jnp.float32)[:, None]
    scaled = scale_col * through
    grad_gate = (scaled * up_val * sig_gate * (1.0 + gate_val * (1.0 - sig_gate))).astype(
        jnp.bfloat16
    )
    grad_up = (scaled * gate_val * sig_gate).astype(jnp.bfloat16)
    weighted = (scale_col * hidden).astype(jnp.bfloat16)
    down_term = lax.dot_general(
        weighted, rows_grad, (((0,), (0,)), ((), ())), preferred_element_type=jnp.float32
    )
    return (grad_gate, grad_up, part_score, down_term)


def local(grad_out, router_score, routing, gate_pre, up_pre, gate_weight, up_weight, down_weight):
    n_expert = lax.axis_size("expert")
    tok_count = grad_out.shape[0]
    width = grad_out.shape[1]
    capacity = tok_count // n_expert + tok_count // (4 * n_expert)
    slot_count = n_expert * capacity
    gate_local = gate_pre[0]
    up_local = up_pre[0]
    down_local = down_weight[0]
    gate_mat = gate_weight[0]
    up_mat = up_weight[0]
    expert_ids = routing[:, 0]
    onehot = (expert_ids[:, None] == jnp.arange(n_expert, dtype=jnp.int32)[None, :]).astype(
        jnp.int32
    )
    before = jnp.cumsum(onehot, axis=0) - onehot
    position = jnp.sum(before * onehot, axis=1)
    slot_index = expert_ids * capacity + position
    send_grad = jnp.zeros((slot_count, width), jnp.bfloat16).at[slot_index].set(grad_out)
    send_score = jnp.zeros((slot_count,), jnp.bfloat16).at[slot_index].set(router_score)
    recv_grad, recv_score = (
        lax.all_to_all(
            send_grad.reshape(n_expert, capacity, width),
            "expert",
            split_axis=0,
            concat_axis=0,
            tiled=True,
        ),
        lax.all_to_all(
            send_score.reshape(n_expert, capacity),
            "expert",
            split_axis=0,
            concat_axis=0,
            tiled=True,
        ),
    )
    recv_grad = recv_grad.reshape(slot_count, width)
    recv_score = recv_score.reshape(slot_count)
    all_grad, all_score = (
        lax.all_gather(recv_grad, "tensor", axis=0, tiled=True),
        lax.all_gather(recv_score, "tensor", axis=0, tiled=True),
    )
    grad_gate, grad_up, part_score, down_sum = expert_rows(
        all_grad, all_score, gate_local, up_local, down_local
    )
    term = lax.dot_general(
        grad_gate, gate_mat, (((1,), (1,)), ((), ())), preferred_element_type=jnp.float32
    )
    mine_grad = lax.psum_scatter(
        (
            term
            + lax.dot_general(
                grad_up, up_mat, (((1,), (1,)), ((), ())), preferred_element_type=jnp.float32
            )
        ).astype(jnp.bfloat16),
        "tensor",
        scatter_dimension=0,
        tiled=True,
    )
    mine_score = lax.psum_scatter(part_score, "tensor", scatter_dimension=0, tiled=True)
    back_grad, back_score = (
        lax.all_to_all(
            mine_grad.reshape(n_expert, capacity, width),
            "expert",
            split_axis=0,
            concat_axis=0,
            tiled=True,
        ),
        lax.all_to_all(
            mine_score.astype(jnp.bfloat16).reshape(n_expert, capacity),
            "expert",
            split_axis=0,
            concat_axis=0,
            tiled=True,
        ),
    )
    grad_tokens = back_grad.reshape(slot_count, width)[slot_index]
    grad_score = back_score.reshape(slot_count)[slot_index]
    grad_down_weight = down_sum.astype(jnp.bfloat16)[None]
    return (grad_tokens, grad_score, grad_down_weight)


def solution(mesh):
    def run(*arrays):
        body = fused_local if fits(mesh, arrays[0], arrays[3]) else local
        return jax.shard_map(
            body,
            mesh=mesh,
            in_specs=(
                P(("expert", "tensor"), None),
                P(("expert", "tensor")),
                P(("expert", "tensor"), None),
                P("expert", None, "tensor"),
                P("expert", None, "tensor"),
                P("expert", None, "tensor"),
                P("expert", None, "tensor"),
                P("expert", "tensor", None),
            ),
            out_specs=(
                P(("expert", "tensor"), None),
                P(("expert", "tensor")),
                P("expert", "tensor", None),
            ),
            check_vma=False,
        )(*arrays)

    return run
```
